32 devices in a mesh: groups: 2 (over y), freq: 4 (over z), src: 2 (over x), vp: 2 (over core).
Axes of the slice: x: 2, y: 2, z: 4, core: 2. Of those that a mesh axis runs over, the one named last changes fastest.
Arguments:
- first_field: float32 [64, 1536, 512], P(('groups', 'src', 'vp'), 'freq'), parts along dimension 0, may hold values from -6 to 6
- onset: int32 [64, 1536], P(('groups', 'src', 'vp'), 'freq'), parts along dimension 0, may hold values from 64 to 447
- kernel: float32 [56, 2, 1536, 1536], P(('groups', 'freq'), None, 'src'), parts along dimension 0, may hold values from -0.4375 to 0.4375
- bin_owner: int32 [24], replicated, may hold values from 0 to 3, as said below
Outputs:
- focusing: float32 [64, 1536, 512], P(('groups', 'src', 'vp'), 'freq'), parts along dimension 0
The draws below stay inside these ranges and needn't reach their ends.
There are 2 independent parts, one for each index of `groups`. The reference program is written for one: setup_inputs(seed, part) draws one part's arguments, and reference() takes and returns one part's arrays. A program takes and returns all parts, laid end to end along the dimension named above; an argument that names none is the same for every part. Nothing has to cross between parts.
Inputs may be any that keep to these rules, and one draw needn't show every extreme that they name: bin_owner never falls; no freq index owns more than 7 bins and one owns exactly 7; the bins of freq index d sit in increasing order in its first slots of kernel, slots d * 7 on.
All inputs are finite; a program needn't handle non-finite values.
Results may differ from the reference program's by a relative error of at most 0.0001.
Values sent between devices are 32-bit elements; how exact they have to be, the bound alone decides.
No kernel may reach another device: no remote copies, remote signals or barrier semaphores. Data moves between devices by JAX's collectives and lax.ppermute only.
A program may use at most 448 MiB of HBM per device.

```python
import math
import jax
import jax.numpy as jnp
from jax import lax

TR = 1536
NT = 512
NF = 24
FIRST_BIN = 4
VP = 32
ITERS = 2
CAP = 7
SLOTS = 28
N_FREQ = 4


def draw_bin_owner(key, part):
    key = jax.random.fold_in(key, 7)
    base = NF // N_FREQ
    extra = NF - base * N_FREQ
    shift = int(extra == 0)
    raw = jax.random.randint(key, (N_FREQ,), 0, 1 << 20, dtype=jnp.int32)
    scores = raw * N_FREQ + jnp.arange(N_FREQ, dtype=jnp.int32)
    order = jnp.argsort(scores, stable=True)
    rank = jnp.argsort(order, stable=True).astype(jnp.int32)
    counts = base + (rank < extra).astype(jnp.int32)
    counts = counts + shift * ((rank == 0).astype(jnp.int32) - (rank == 1).astype(jnp.int32))
    bounds = jnp.cumsum(counts)
    bin_index = jnp.arange(NF, dtype=jnp.int32)
    owner = jnp.sum((bounds[None, :] <= bin_index[:, None]).astype(jnp.int32), axis=1)
    return owner.astype(jnp.int32)


def touch_ends(values, stream_key, least, high):
    longest = values.shape.index(max(values.shape))
    spots = []
    for shift in (0, 1):
        where = [jax.random.randint(jax.random.fold_in(stream_key, axis), (), 0, length) for axis, length in enumerate(values.shape)]
        where[longest] = (where[longest] + shift) % values.shape[longest]
        spots.append(tuple(where))
    return values.at[spots[0]].set(least).at[spots[1]].set(high)


def steps_of(key, dims, pieces, smallest, high):
    loudness = 1.0
    for dim, shards_of in pieces:
        heights = jax.random.uniform(jax.random.fold_in(jax.random.fold_in(key, 6), dim), (shards_of,), jnp.float32, smallest / len(pieces), high / len(pieces))
        loudness = loudness * jnp.repeat(jnp.exp(heights), dims[dim] // shards_of).reshape((-1,) + (1,) * (len(dims) - 1 - dim))
    return loudness


def gaussian(rng, extent, spread, limit, shards=(), kind=jnp.bfloat16):
    level = steps_of(rng, extent, shards, -0.22, 0.18) if shards else 1.0
    values = jax.random.normal(rng, extent, jnp.float32) * spread * level
    return jnp.minimum(jnp.maximum(values, -limit), limit).astype(kind)


def setup_inputs(seed: int = 0, part: int = 0) -> dict:
    seeds = jax.random.split(jax.random.key(seed), 5)
    part_splits = jax.random.split(jax.random.fold_in(seeds[4], part), 5)
    return {
        "first_field": gaussian(part_splits[0], (VP, TR, NT), 1.0, 6.0, ((0, 4), (1, 4)), jnp.float32),
        "onset": touch_ends(jax.random.randint(part_splits[1], (VP, TR), NT // 8, 7 * NT // 8), jax.random.fold_in(part_splits[1], 1), NT // 8, (7 * NT // 8) - 1).astype(jnp.int32),
        "kernel": gaussian(part_splits[2], (SLOTS, 2, TR, TR), (TR // 8) ** -0.5, 0.4375, ((0, 4), (2, 2)), jnp.float32),
        "bin_owner": draw_bin_owner(jax.random.fold_in(seeds[4], 71), part),
    }


highest_precision = lax.Precision.HIGHEST


def reference(first_field, onset, kernel, bin_owner):
    bin_index = jnp.arange(NF, dtype=jnp.int32)
    earlier = (bin_owner[:, None] == bin_owner[None, :]) & (bin_index[None, :] < bin_index[:, None])
    rank = jnp.sum(earlier.astype(jnp.int32), axis=1)
    slot_of = (bin_owner * CAP + rank).astype(jnp.int32)
    sample = jnp.arange(NT, dtype=jnp.int32)
    phase = (sample[:, None] * (FIRST_BIN + bin_index)[None, :]) % NT
    angle = phase.astype(jnp.float32) * (2.0 * math.pi / NT)
    cosine = jnp.cos(angle)
    sine = jnp.sin(angle)
    scale = 2.0 / NT
    keep = (sample[None, None, :] < onset[:, :, None]).astype(jnp.float32)

    def spectrum_of(field):
        real_part = jnp.einsum("vrt,tb->bvr", field, cosine, precision=highest_precision)
        imag_part = -jnp.einsum("vrt,tb->bvr", field, sine, precision=highest_precision)
        return jnp.stack([real_part, imag_part], axis=1)

    def inverse_of(spectrum):
        first = jnp.einsum("bvr,tb->vrt", spectrum[:, 0], cosine * scale, precision=highest_precision)
        second = jnp.einsum("bvr,tb->vrt", spectrum[:, 1], sine * scale, precision=highest_precision)
        return first - second

    def convolve(spectrum):
        def one_bin(item):
            slot, pair = item
            block = lax.dynamic_index_in_dim(kernel, slot, 0, keepdims=False)

            def product(left, right):
                return jnp.einsum("vr,sr->vs", left, right, precision=highest_precision)

            real_out = product(pair[0], block[0]) - product(pair[1], block[1])
            imag_out = product(pair[1], block[0]) + product(pair[0], block[1])
            return jnp.stack([real_out, imag_out])

        return lax.map(one_bin, (slot_of, spectrum))

    def correlate(spectrum):
        def one_bin(item):
            slot, pair = item
            block = lax.dynamic_index_in_dim(kernel, slot, 0, keepdims=False)

            def product(left, right):
                return jnp.einsum("vs,sr->vr", left, right, precision=highest_precision)

            real_out = product(pair[0], block[0]) + product(pair[1], block[1])
            imag_out = product(pair[1], block[0]) - product(pair[0], block[1])
            return jnp.stack([real_out, imag_out])

        return lax.map(one_bin, (slot_of, spectrum))

    focusing = first_field
    for sweep in range(ITERS):
        down = keep * inverse_of(convolve(spectrum_of(focusing)))
        focusing = first_field + keep * inverse_of(correlate(spectrum_of(down)))
    return focusing
```

```python
import math

import jax
import jax.numpy as jnp
from jax import lax
from jax.experimental import pallas as pl
from jax.experimental.pallas import tpu as pltpu
from jax.sharding import PartitionSpec as P

NT = 512
NF = 24
FIRST_BIN = 4
ITERS = 2
PARTS = 2
F32 = jnp.float32
BF16 = jnp.bfloat16
LIMIT = 56 << 20


highest_precision = lax.Precision.HIGHEST


def slot_tables(bin_owner, slots_here, total_slots):
    bin_index = jnp.arange(NF, dtype=jnp.int32)
    earlier = (bin_owner[:, None] == bin_owner[None, :]) & (bin_index[None, :] < bin_index[:, None])
    rank = jnp.sum(earlier.astype(jnp.int32), axis=1)
    slot_of = bin_owner * slots_here + rank
    onehot = (slot_of[:, None] == jnp.arange(total_slots, dtype=jnp.int32)[None, :]).astype(
        jnp.float32
    )
    sample = jnp.arange(NT, dtype=jnp.int32)
    phase = sample[:, None] * (FIRST_BIN + bin_index)[None, :] % NT
    angle = phase.astype(jnp.float32) * (2.0 * math.pi / NT)
    cosine = jnp.dot(jnp.cos(angle), onehot, precision=highest_precision)
    sine = jnp.dot(jnp.sin(angle), onehot, precision=highest_precision)
    scale = 2.0 / NT
    forward_table = jnp.stack([cosine, -sine], axis=2).reshape(NT, 2 * total_slots)
    inverse_table = jnp.stack([cosine.T * scale, -(sine.T * scale)], axis=1).reshape(
        2 * total_slots, NT
    )
    return (forward_table, inverse_table)


def convolve_pairs(spectrum, kernel_view):

    def product(left, right):
        return jnp.einsum("edcvr,cfsdr->efcvs", left, right, precision=highest_precision)

    real_out = product(spectrum[:, :, :, 0], kernel_view[:, 0]) - product(
        spectrum[:, :, :, 1], kernel_view[:, 1]
    )
    imag_out = product(spectrum[:, :, :, 1], kernel_view[:, 0]) + product(
        spectrum[:, :, :, 0], kernel_view[:, 1]
    )
    return jnp.stack([real_out, imag_out], axis=3)


def correlate_pairs(spectrum, kernel_view):

    def product(left, right):
        return jnp.einsum("efcvr,cfrdq->edcvq", left, right, precision=highest_precision)

    real_out = product(spectrum[:, :, :, 0], kernel_view[:, 0]) + product(
        spectrum[:, :, :, 1], kernel_view[:, 1]
    )
    imag_out = product(spectrum[:, :, :, 1], kernel_view[:, 0]) - product(
        spectrum[:, :, :, 0], kernel_view[:, 1]
    )
    return jnp.stack([real_out, imag_out], axis=3)


def local_general(first_field, onset, kernel, bin_owner):
    slots_here = kernel.shape[0]
    freq_count = lax.axis_size("freq")
    src_count = lax.axis_size("src")
    sub_blocks = freq_count // src_count
    total_slots = slots_here * freq_count
    forward_table, inverse_table = slot_tables(bin_owner, slots_here, total_slots)
    points = first_field.shape[0]
    traces = first_field.shape[1]
    kernel_view = kernel.reshape(slots_here, 2, sub_blocks, traces, freq_count, traces)
    sample = jnp.arange(NT, dtype=jnp.int32)
    keep = (sample[None, None, :] < onset[:, :, None]).astype(jnp.float32)

    def to_bins(field):
        spectrum = jnp.einsum("vrt,tc->cvr", field, forward_table, precision=highest_precision)
        spectrum = spectrum.reshape(freq_count, slots_here, 2, points, traces)
        return lax.all_to_all(spectrum, "freq", split_axis=0, concat_axis=0, tiled=True)

    def to_time(spectrum):
        regrouped = lax.all_to_all(spectrum, "freq", split_axis=0, concat_axis=0, tiled=True)
        flat = regrouped.reshape(2 * total_slots, points, traces)
        return jnp.einsum("cvr,ct->vrt", flat, inverse_table, precision=highest_precision)

    def widen(spectrum):
        return lax.all_gather(spectrum[None], "src", axis=0, tiled=True)

    focusing = first_field
    for sweep in range(ITERS):
        widened = widen(to_bins(focusing))
        direct = convolve_pairs(widened, kernel_view)
        direct = lax.all_to_all(direct, "src", split_axis=0, concat_axis=0, tiled=True)
        direct = direct.reshape(freq_count, slots_here, 2, points, traces)
        down = keep * to_time(direct)
        spectrum = to_bins(down)
        local_part = lax.dynamic_slice_in_dim(
            widen(spectrum), lax.axis_index("src") * sub_blocks, sub_blocks, 1
        )
        partial_terms = correlate_pairs(local_part, kernel_view)
        summed = lax.psum_scatter(partial_terms, "src", scatter_dimension=0, tiled=True)
        summed = summed.reshape(freq_count, slots_here, 2, points, traces)
        focusing = first_field + keep * to_time(summed)
    return focusing


def split(x):
    high = x.astype(BF16)
    return high, (x - high.astype(F32)).astype(BF16)


def stacked_split(x):
    high, low = split(x)
    return jnp.concatenate([high.astype(F32), low.astype(F32)], axis=0).astype(BF16)


def dot_nt(a, b):
    return lax.dot_general(a, b, (((1,), (1,)), ((), ())), preferred_element_type=F32)


def dot_nn(a, b):
    return lax.dot_general(a, b, (((1,), (0,)), ((), ())), preferred_element_type=F32)


def dot_tn(a, b):
    return lax.dot_general(a, b, (((0,), (0,)), ((), ())), preferred_element_type=F32)


def three_products(dot, both, k):
    high, low = split(k)
    rows = both.shape[0] // 2
    p = dot(both, high)
    return p[:rows] + p[rows:] + dot(both[:rows], low)


def tables(bin_owner, me, slots, freqs):
    owner = jnp.bitwise_xor(me, jnp.arange(freqs, dtype=jnp.int32))
    start = jnp.sum((bin_owner[None, :] < owner[:, None]).astype(jnp.int32), axis=1)
    count = jnp.sum((bin_owner[None, :] == owner[:, None]).astype(jnp.int32), axis=1)
    slot = jnp.arange(slots, dtype=jnp.int32)
    index = start[:, None] + slot[None, :] + FIRST_BIN
    valid = slot[None, :] < count[:, None]
    sample = jnp.arange(NT, dtype=jnp.int32)
    phase = index[:, :, None] * sample % NT
    angle = phase.astype(F32) * (2.0 * math.pi / NT)
    pair = jnp.stack([jnp.cos(angle), -jnp.sin(angle)], axis=2)
    return jnp.where(valid[:, :, None, None], pair, 0.0).reshape(freqs * slots * 2, NT)


def whole(shape):
    zeros = (0,) * len(shape)
    return pl.BlockSpec(shape, lambda *_: zeros)


def spectrum_kernel(points, parts, u, table, *rest):
    outs, scratch, both = rest[:-2], rest[-2], rest[-1]
    v = pl.program_id(0)

    @pl.when(v == 0)
    def _():
        both[...] = stacked_split(table[...])

    rows = table.shape[0]
    high, low = split(u[0])
    p = dot_nt(both[...], high)
    s = p[:rows] + p[rows:] + dot_nt(table[...].astype(BF16), low)
    set_point(scratch, v, points, s)

    @pl.when(v == points - 1)
    def _():
        put_pieces(scratch, outs, points, parts)


def set_point(scratch, v, points, value):
    for i in range(scratch.shape[0]):
        scratch[i, pl.ds(v, value.shape[0], stride=points), :] = value[:, 128 * i : 128 * i + 128]


def get_point(scratch, v, points):
    tiles = range(scratch.shape[0])
    rows = scratch.shape[1] // points
    return jnp.concatenate([scratch[i, pl.ds(v, rows, stride=points), :] for i in tiles], axis=1)


def rows_scratch(rows, traces):
    return pltpu.VMEM((traces // 128, rows, 128), F32)


def put_pieces(scratch, outs, points, parts, extra=None):
    height = 2 * points
    row = 0
    slots = sum(parts)
    for k in range(4):
        done = 0
        for n, size in enumerate(parts):
            for j in range(size):
                row = (k * slots + done + j) * height
                for i in range(scratch.shape[0]):
                    lanes = slice(128 * i, 128 * i + 128)
                    value = scratch[i, row : row + height, :]
                    if extra is not None:
                        value = value + extra[4 * n + k][j, :, lanes]
                    outs[4 * n + k][j, :, lanes] = value
            done += size


def take_pieces(scratch, ins, points, parts):
    height = 2 * points
    slots = sum(parts)
    for k in range(4):
        done = 0
        for n, size in enumerate(parts):
            for j in range(size):
                row = (k * slots + done + j) * height
                for i in range(scratch.shape[0]):
                    lanes = slice(128 * i, 128 * i + 128)
                    scratch[i, row : row + height, :] = ins[4 * n + k][j, :, lanes]
            done += size


def piece_shapes(parts, height, traces):
    return [jax.ShapeDtypeStruct((size, height, traces), F32) for size in parts for _ in range(4)]


def spectrum(field, table, parts):
    points, traces, _ = field.shape
    rows = table.shape[0]
    shapes = piece_shapes(parts, 2 * points, traces)

    def kernel(*refs):
        spectrum_kernel(points, parts, *refs)

    return pl.pallas_call(
        kernel,
        grid=(points,),
        in_specs=[pl.BlockSpec((1, traces, NT), lambda v: (v, 0, 0)), whole(table.shape)],
        out_specs=[whole(s.shape) for s in shapes],
        out_shape=shapes,
        scratch_shapes=[rows_scratch(rows * points, traces), pltpu.VMEM((2 * rows, NT), BF16)],
        compiler_params=pltpu.CompilerParams(vmem_limit_bytes=LIMIT),
    )(field, table)


def inverse_factor(table, axis):
    high, low = split(table * (2.0 / NT))
    third = table.shape[axis] // 3
    at = lax.broadcasted_iota(jnp.int32, table.shape, axis)
    middle = (at >= third) & (at < 2 * third)
    return jnp.where(middle, low.astype(F32), high.astype(F32)).astype(BF16)


def field_factor(x):
    high, low = split(x)
    high, low = high.astype(F32), low.astype(F32)
    return jnp.concatenate([high, high, low], axis=0).astype(BF16)


def window(pieces, table, onset, parts, extra=None):
    points, traces = onset.shape
    rows = table.shape[0]
    shapes = piece_shapes(parts, 2 * points, traces)
    count = len(shapes)
    extra = list(extra) if extra is not None else []
    backward = jnp.concatenate([table.T] * 3, axis=1)

    def kernel(*refs):
        ins, refs = refs[:count], refs[count:]
        more, refs = refs[: len(extra)], refs[len(extra) :]
        table_ref, back_ref, onset_ref = refs[:3]
        outs, (x_scratch, y_scratch) = refs[3:-2], refs[-2:]
        take_pieces(x_scratch, ins, points, parts)
        forward = stacked_split(table_ref[...])
        back = inverse_factor(back_ref[...], 1)
        sample = lax.broadcasted_iota(jnp.int32, (NT, traces), 0)
        for v in range(points):
            x = field_factor(get_point(x_scratch, v, points))
            down = jnp.where(sample < onset_ref[v : v + 1, :], dot_nn(back, x), 0.0)
            set_point(y_scratch, v, points, transform(forward, table_ref, down))
        put_pieces(y_scratch, outs, points, parts, more if extra else None)

    def transform(forward, table_ref, down):
        high, low = split(down)
        p = dot_nn(forward, high)
        return p[:rows] + p[rows:] + dot_nn(table_ref[...].astype(BF16), low)

    return pl.pallas_call(
        kernel,
        out_shape=shapes,
        scratch_shapes=[rows_scratch(rows * points, traces)] * 2,
        compiler_params=pltpu.CompilerParams(vmem_limit_bytes=LIMIT),
    )(*pieces, *extra, table, backward, onset)


def finish(pieces, table, onset, field, parts):
    points, traces = onset.shape
    rows = table.shape[0]
    factor = jnp.concatenate([table] * 3, axis=0)
    count = len(pieces)

    def kernel(*refs):
        ins = refs[:count]
        factor_ref, onset_ref, field_ref, out_ref, scratch = refs[count:]
        v = pl.program_id(0)

        @pl.when(v == 0)
        def _():
            take_pieces(scratch, ins, points, parts)

        x = field_factor(get_point(scratch, v, points))
        g = dot_tn(x, inverse_factor(factor_ref[...], 0))
        sample = lax.broadcasted_iota(jnp.int32, (traces, NT), 1)
        out_ref[0] = field_ref[0] + jnp.where(sample < onset_ref[0], g, 0.0)

    block = pl.BlockSpec((1, traces, NT), lambda v: (v, 0, 0))
    return pl.pallas_call(
        kernel,
        grid=(points,),
        in_specs=[whole(p.shape) for p in pieces]
        + [whole(factor.shape), pl.BlockSpec((1, traces, 1), lambda v: (v, 0, 0)), block],
        out_specs=block,
        out_shape=jax.ShapeDtypeStruct(field.shape, F32),
        scratch_shapes=[rows_scratch(rows * points, traces)],
        compiler_params=pltpu.CompilerParams(vmem_limit_bytes=LIMIT),
    )(*pieces, factor, onset[:, :, None], field)


def put_rows(both, both_turned, at, lanes, piece, sign):
    half = piece.shape[0] // 2
    rows = both.shape[0] // 2
    re, im = piece[:half], piece[half:]
    turned = jnp.concatenate([-im, re] if sign > 0 else [im, -re], axis=0)
    for target, value in ((both, piece), (both_turned, turned)):
        high, low = split(value)
        target[pl.ds(at, 2 * half), lanes] = high
        target[pl.ds(pl.multiple_of(rows + at, 16), 2 * half), lanes] = low


def convolve(partners, kernel, place, offset):
    _, slots, height, traces = partners[0].shape
    quarter = kernel.shape[2] // 2
    line = kernel.shape[3]

    def body(place_ref, a, b, c, d, k, *rest):
        outs, (both, turned, g) = rest[:4], rest[4:]
        me = place_ref[0]
        for i in range(4):
            lanes = pl.ds(pl.multiple_of((me ^ i) * traces, 128), traces)
            for p, ref in enumerate((a, b, c, d)):
                put_rows(both, turned, p * height, lanes, ref[i, 0], 1)
        g[...] = three_products(dot_nt, both[...], k[0, 0])
        g[...] += three_products(dot_nt, turned[...], k[0, 1])
        for i in range(4):
            outs[i][0] = g[pl.ds(pl.multiple_of((me ^ i) * height, 16), height), :]

    shape = jax.ShapeDtypeStruct((slots, height, quarter), F32)
    return pl.pallas_call(
        body,
        grid_spec=pltpu.PrefetchScalarGridSpec(
            num_scalar_prefetch=1,
            grid=(slots,),
            in_specs=[pl.BlockSpec((4, 1, height, traces), lambda j, s: (0, j, 0, 0))] * 4
            + [pl.BlockSpec((1, 2, quarter, line), lambda j, s: (j + offset, 0, s[1], 0))],
            out_specs=[pl.BlockSpec((1, height, quarter), lambda j, s: (j, 0, 0))] * 4,
            scratch_shapes=[
                pltpu.VMEM((8 * height, line), BF16),
                pltpu.VMEM((8 * height, line), BF16),
                pltpu.VMEM((4 * height, quarter), F32),
            ],
        ),
        out_shape=[shape] * 4,
        compiler_params=pltpu.CompilerParams(vmem_limit_bytes=LIMIT),
    )(place, *partners, kernel)


def correlate(pieces, kernel, place, offset, traces):
    slots, height, quarter = pieces[0].shape
    line = kernel.shape[3]

    def body(place_ref, a, b, c, d, k, own, other, sibling, both, turned, h):
        me = place_ref[0]
        for i, ref in enumerate((a, b, c, d)):
            at = pl.multiple_of((me ^ i) * height, 16)
            put_rows(both, turned, at, slice(None), ref[0], -1)
        h[...] = three_products(dot_nn, both[...], k[0, 0])
        h[...] += three_products(dot_nn, turned[...], k[0, 1])
        for i in range(4):
            lanes = pl.ds(pl.multiple_of((me ^ i) * traces, 128), traces)
            own[i, 0] = h[:height, lanes]
            other[i, 0] = h[height : 2 * height, lanes]
            sibling[0, i, 0] = h[2 * height : 3 * height, lanes]
            sibling[1, i, 0] = h[3 * height :, lanes]

    one = jax.ShapeDtypeStruct((4, slots, height, traces), F32)
    two = jax.ShapeDtypeStruct((2, 4, slots, height, traces), F32)
    one_block = pl.BlockSpec((4, 1, height, traces), lambda j, s: (0, j, 0, 0))
    two_block = pl.BlockSpec((2, 4, 1, height, traces), lambda j, s: (0, 0, j, 0, 0))
    return pl.pallas_call(
        body,
        grid_spec=pltpu.PrefetchScalarGridSpec(
            num_scalar_prefetch=1,
            grid=(slots,),
            in_specs=[pl.BlockSpec((1, height, quarter), lambda j, s: (j, 0, 0))] * 4
            + [pl.BlockSpec((1, 2, quarter, line), lambda j, s: (j + offset, 0, s[1], 0))],
            out_specs=[one_block, one_block, two_block],
            scratch_shapes=[
                pltpu.VMEM((8 * height, quarter), BF16),
                pltpu.VMEM((8 * height, quarter), BF16),
                pltpu.VMEM((4 * height, line), F32),
            ],
        ),
        out_shape=[one, one, two],
        compiler_params=pltpu.CompilerParams(vmem_limit_bytes=LIMIT),
    )(place, *pieces, kernel)


def exchange(pieces):
    out = [pieces[0]]
    for k in range(1, 4):
        out.append(lax.ppermute(pieces[k], "freq", [(f, f ^ k) for f in range(4)]))
    return out


def swap(x, axis):
    return lax.ppermute(x, axis, [(0, 1), (1, 0)])


def local_kernels(first_field, onset, kernel, bin_owner):
    slots = kernel.shape[0]
    traces = first_field.shape[1]
    parts = [slots // PARTS + (n < slots % PARTS) for n in range(PARTS)]
    offsets = [sum(parts[:n]) for n in range(PARTS)]
    me = lax.axis_index("freq").astype(jnp.int32)
    core = lax.axis_index("vp").astype(jnp.int32)
    place = jnp.stack([me, core])
    table = tables(bin_owner, me, slots, 4)
    moves = []
    for f in range(4):
        for x in range(2):
            for c in range(2):
                source = ((2 * x + c) * 2 + (x ^ (f & 1))) * 2 + (c ^ (f >> 1))
                moves.append((source, (f * 2 + x) * 2 + c))
    onset_inner = lax.ppermute(onset, ("freq", "src", "vp"), moves)

    def part_of(pieces, n):
        return pieces[4 * n : 4 * n + 4]

    def conv_part(pieces, n):
        own = jnp.stack(exchange(pieces))
        other = swap(own, "src")
        sibling = swap(own, "vp")
        across = swap(other, "vp")
        return convolve((own, other, sibling, across), kernel, place, offsets[n])

    def corr_part(pieces, n):
        own, other, sibling = correlate(exchange(pieces), kernel, place, offsets[n], traces)
        from_sibling = swap(sibling, "vp")
        from_other = swap(other + from_sibling[1], "src")
        total = own + from_sibling[0] + from_other
        return exchange([total[k] for k in range(4)])

    first = spectrum(first_field, table, parts)
    pieces = first
    for sweep in range(ITERS):
        out = []
        for n in range(PARTS):
            out += exchange(conv_part(part_of(pieces, n), n))
        inner = window(out, table, onset_inner, parts)
        out = []
        for n in range(PARTS):
            out += corr_part(part_of(inner, n), n)
        if sweep < ITERS - 1:
            pieces = window(out, table, onset, parts, first)
    return finish(out, table, onset, first_field, parts)


def local(first_field, onset, kernel, bin_owner):
    points, traces, samples = first_field.shape
    quarter = kernel.shape[2] // lax.axis_size("vp")
    sizes = tuple(lax.axis_size(name) for name in ("freq", "src", "vp"))
    fits = sizes == (4, 2, 2) and points == 8 and samples == NT
    if fits and traces % 128 == 0 and quarter == traces and kernel.shape[3] == 4 * traces:
        return local_kernels(first_field, onset, kernel, bin_owner)
    return local_general(first_field, onset, kernel, bin_owner)


def solution(mesh):
    in_specs = (
        P(("groups", "src", "vp"), "freq", None),
        P(("groups", "src", "vp"), "freq"),
        P(("groups", "freq"), None, "src", None),
        P(),
    )
    out_specs = P(("groups", "src", "vp"), "freq", None)
    return jax.shard_map(local, mesh=mesh, in_specs=in_specs, out_specs=out_specs, check_vma=False)
```

```python
import math

import jax
import jax.numpy as jnp
from jax import lax
from jax.experimental import pallas as pl
from jax.experimental.pallas import tpu as pltpu
from jax.sharding import PartitionSpec as P

NT = 512
NF = 24
FIRST_BIN = 4
ITERS = 2
PARTS = 2
F32 = jnp.float32
BF16 = jnp.bfloat16
LIMIT = 12 << 20


highest_precision = lax.Precision.HIGHEST


def slot_tables(bin_owner, slots_here, total_slots):
    bin_index = jnp.arange(NF, dtype=jnp.int32)
    earlier = (bin_owner[:, None] == bin_owner[None, :]) & (bin_index[None, :] < bin_index[:, None])
    rank = jnp.sum(earlier.astype(jnp.int32), axis=1)
    slot_of = bin_owner * slots_here + rank
    onehot = (slot_of[:, None] == jnp.arange(total_slots, dtype=jnp.int32)[None, :]).astype(
        jnp.float32
    )
    sample = jnp.arange(NT, dtype=jnp.int32)
    phase = sample[:, None] * (FIRST_BIN + bin_index)[None, :] % NT
    angle = phase.astype(jnp.float32) * (2.0 * math.pi / NT)
    cosine = jnp.dot(jnp.cos(angle), onehot, precision=highest_precision)
    sine = jnp.dot(jnp.sin(angle), onehot, precision=highest_precision)
    scale = 2.0 / NT
    forward_table = jnp.stack([cosine, -sine], axis=2).reshape(NT, 2 * total_slots)
    inverse_table = jnp.stack([cosine.T * scale, -(sine.T * scale)], axis=1).reshape(
        2 * total_slots, NT
    )
    return (forward_table, inverse_table)


def convolve_pairs(spectrum, kernel_view):

    def product(left, right):
        return jnp.einsum("edcvr,cfsdr->efcvs", left, right, precision=highest_precision)

    real_out = product(spectrum[:, :, :, 0], kernel_view[:, 0]) - product(
        spectrum[:, :, :, 1], kernel_view[:, 1]
    )
    imag_out = product(spectrum[:, :, :, 1], kernel_view[:, 0]) + product(
        spectrum[:, :, :, 0], kernel_view[:, 1]
    )
    return jnp.stack([real_out, imag_out], axis=3)


def correlate_pairs(spectrum, kernel_view):

    def product(left, right):
        return jnp.einsum("efcvr,cfrdq->edcvq", left, right, precision=highest_precision)

    real_out = product(spectrum[:, :, :, 0], kernel_view[:, 0]) + product(
        spectrum[:, :, :, 1], kernel_view[:, 1]
    )
    imag_out = product(spectrum[:, :, :, 1], kernel_view[:, 0]) - product(
        spectrum[:, :, :, 0], kernel_view[:, 1]
    )
    return jnp.stack([real_out, imag_out], axis=3)


def local_general(first_field, onset, kernel, bin_owner):
    slots_here = kernel.shape[0]
    freq_count = lax.axis_size("freq")
    src_count = lax.axis_size("src")
    sub_blocks = freq_count // src_count
    total_slots = slots_here * freq_count
    forward_table, inverse_table = slot_tables(bin_owner, slots_here, total_slots)
    points = first_field.shape[0]
    traces = first_field.shape[1]
    kernel_view = kernel.reshape(slots_here, 2, sub_blocks, traces, freq_count, traces)
    sample = jnp.arange(NT, dtype=jnp.int32)
    keep = (sample[None, None, :] < onset[:, :, None]).astype(jnp.float32)

    def to_bins(field):
        spectrum = jnp.einsum("vrt,tc->cvr", field, forward_table, precision=highest_precision)
        spectrum = spectrum.reshape(freq_count, slots_here, 2, points, traces)
        return lax.all_to_all(spectrum, "freq", split_axis=0, concat_axis=0, tiled=True)

    def to_time(spectrum):
        regrouped = lax.all_to_all(spectrum, "freq", split_axis=0, concat_axis=0, tiled=True)
        flat = regrouped.reshape(2 * total_slots, points, traces)
        return jnp.einsum("cvr,ct->vrt", flat, inverse_table, precision=highest_precision)

    def widen(spectrum):
        return lax.all_gather(spectrum[None], "src", axis=0, tiled=True)

    focusing = first_field
    for sweep in range(ITERS):
        widened = widen(to_bins(focusing))
        direct = convolve_pairs(widened, kernel_view)
        direct = lax.all_to_all(direct, "src", split_axis=0, concat_axis=0, tiled=True)
        direct = direct.reshape(freq_count, slots_here, 2, points, traces)
        down = keep * to_time(direct)
        spectrum = to_bins(down)
        local_part = lax.dynamic_slice_in_dim(
            widen(spectrum), lax.axis_index("src") * sub_blocks, sub_blocks, 1
        )
        partial_terms = correlate_pairs(local_part, kernel_view)
        summed = lax.psum_scatter(partial_terms, "src", scatter_dimension=0, tiled=True)
        summed = summed.reshape(freq_count, slots_here, 2, points, traces)
        focusing = first_field + keep * to_time(summed)
    return focusing


def split(x):
    high = x.astype(BF16)
    return high, (x - high.astype(F32)).astype(BF16)


def stacked_split(x):
    high, low = split(x)
    return jnp.concatenate([high.astype(F32), low.astype(F32)], axis=0).astype(BF16)


def dot_nt(a, b):
    return lax.dot_general(a, b, (((1,), (1,)), ((), ())), preferred_element_type=F32)


def dot_nn(a, b):
    return lax.dot_general(a, b, (((1,), (0,)), ((), ())), preferred_element_type=F32)


def dot_tn(a, b):
    return lax.dot_general(a, b, (((0,), (0,)), ((), ())), preferred_element_type=F32)


def three_products(dot, both, high, low):
    rows = both.shape[0] // 2
    p = dot(both, high)
    return p[:rows] + p[rows:] + dot(both[:rows], low)


def tables(bin_owner, me, slots, freqs):
    owner = jnp.bitwise_xor(me, jnp.arange(freqs, dtype=jnp.int32))
    start = jnp.sum((bin_owner[None, :] < owner[:, None]).astype(jnp.int32), axis=1)
    count = jnp.sum((bin_owner[None, :] == owner[:, None]).astype(jnp.int32), axis=1)
    slot = jnp.arange(slots, dtype=jnp.int32)
    index = start[:, None] + slot[None, :] + FIRST_BIN
    valid = slot[None, :] < count[:, None]
    sample = jnp.arange(NT, dtype=jnp.int32)
    phase = index[:, :, None] * sample % NT
    angle = phase.astype(F32) * (2.0 * math.pi / NT)
    pair = jnp.stack([jnp.cos(angle), -jnp.sin(angle)], axis=2)
    return jnp.where(valid[:, :, None, None], pair, 0.0).reshape(freqs * slots * 2, NT)


def OUT(shape):
    return pltpu.VMEM(shape.shape, shape.dtype)


ON_CHIP = pl.BlockSpec(memory_space=pltpu.VMEM)


def on_chip(values):
    return [pltpu.with_memory_space_constraint(value, pltpu.VMEM) for value in values]


def load(kernel, place):
    slots, pair, sources, line = kernel.shape
    quarter = sources // 2
    shape = (slots, pair, quarter, line)

    def body(place_ref, k, high_ref, low_ref, buffer, sems):
        def copy(n):
            rows = pl.ds(pl.multiple_of(place_ref[1] * quarter, 8), quarter)
            source = k.at[n // pair, n % pair, rows, :]
            return pltpu.make_async_copy(source, buffer.at[n % 3], sems.at[n % 3])

        copy(0).start()
        copy(1).start()
        for n in range(slots * pair):
            if n + 2 < slots * pair:
                copy(n + 2).start()
            copy(n).wait()
            high, low = split(buffer[n % 3])
            high_ref[n // pair, n % pair] = high
            low_ref[n // pair, n % pair] = low

    return pl.pallas_call(
        body,
        in_specs=[pl.BlockSpec(memory_space=pltpu.SMEM), pl.BlockSpec(memory_space=pl.ANY)],
        out_specs=[ON_CHIP, ON_CHIP],
        out_shape=[pltpu.VMEM(shape, BF16)] * 2,
        scratch_shapes=[pltpu.VMEM((3, quarter, line), F32), pltpu.SemaphoreType.DMA((3,))],
        compiler_params=pltpu.CompilerParams(vmem_limit_bytes=LIMIT),
    )(place, kernel)


def whole(shape):
    zeros = (0,) * len(shape)
    return pl.BlockSpec(shape, lambda *_: zeros)


def spectrum_kernel(points, parts, u, table, *rest):
    outs, scratch, both = rest[:-2], rest[-2], rest[-1]
    v = pl.program_id(0)

    @pl.when(v == 0)
    def _():
        both[...] = stacked_split(table[...])

    rows = table.shape[0]
    high, low = split(u[0])
    p = dot_nt(both[...], high)
    s = p[:rows] + p[rows:] + dot_nt(table[...].astype(BF16), low)
    set_point(scratch, v, points, s)

    @pl.when(v == points - 1)
    def _():
        put_pieces(scratch, outs, points, parts)


def set_point(scratch, v, points, value):
    for i in range(scratch.shape[0]):
        scratch[i, pl.ds(v, value.shape[0], stride=points), :] = value[:, 128 * i : 128 * i + 128]


def get_point(scratch, v, points):
    tiles = range(scratch.shape[0])
    rows = scratch.shape[1] // points
    return jnp.concatenate([scratch[i, pl.ds(v, rows, stride=points), :] for i in tiles], axis=1)


def rows_scratch(rows, traces):
    return pltpu.VMEM((traces // 128, rows, 128), F32)


def put_pieces(scratch, outs, points, parts, extra=None):
    height = 2 * points
    row = 0
    slots = sum(parts)
    for k in range(4):
        done = 0
        for n, size in enumerate(parts):
            for j in range(size):
                row = (k * slots + done + j) * height
                for i in range(scratch.shape[0]):
                    lanes = slice(128 * i, 128 * i + 128)
                    value = scratch[i, row : row + height, :]
                    if extra is not None:
                        value = value + extra[4 * n + k][j, :, lanes]
                    outs[4 * n + k][j, :, lanes] = value
            done += size


def take_pieces(scratch, ins, points, parts):
    height = 2 * points
    slots = sum(parts)
    for k in range(4):
        done = 0
        for n, size in enumerate(parts):
            for j in range(size):
                row = (k * slots + done + j) * height
                for i in range(scratch.shape[0]):
                    lanes = slice(128 * i, 128 * i + 128)
                    scratch[i, row : row + height, :] = ins[4 * n + k][j, :, lanes]
            done += size


def piece_shapes(parts, height, traces):
    return [jax.ShapeDtypeStruct((size, height, traces), F32) for size in parts for _ in range(4)]


def spectrum(field, table, parts):
    points, traces, _ = field.shape
    rows = table.shape[0]
    shapes = piece_shapes(parts, 2 * points, traces)

    def kernel(*refs):
        spectrum_kernel(points, parts, *refs)

    return pl.pallas_call(
        kernel,
        grid=(points,),
        in_specs=[pl.BlockSpec((1, traces, NT), lambda v: (v, 0, 0)), whole(table.shape)],
        out_specs=[whole(s.shape) for s in shapes],
        out_shape=shapes,
        scratch_shapes=[rows_scratch(rows * points, traces), pltpu.VMEM((2 * rows, NT), BF16)],
        compiler_params=pltpu.CompilerParams(vmem_limit_bytes=LIMIT),
    )(field, table)


def inverse_factor(table):
    high, low = split(table * (2.0 / NT))
    high, low = high.astype(F32), low.astype(F32)
    return jnp.concatenate([high, low, high], axis=0)


def field_factor(x):
    high, low = split(x)
    high, low = high.astype(F32), low.astype(F32)
    return jnp.concatenate([high, high, low], axis=0).astype(BF16)


def window(pieces, table, onset, parts, extra=None):
    points, traces = onset.shape
    rows = table.shape[0]
    shapes = piece_shapes(parts, 2 * points, traces)
    count = len(shapes)
    extra = list(extra) if extra is not None else []

    def kernel(*refs):
        ins, refs = refs[:count], refs[count:]
        more, refs = refs[: len(extra)], refs[len(extra) :]
        table_ref, onset_ref = refs[:2]
        outs, (x_scratch, y_scratch) = refs[2:-2], refs[-2:]
        take_pieces(x_scratch, ins, points, parts)
        forward = stacked_split(table_ref[...])
        back = inverse_factor(table_ref[...]).T.astype(BF16)
        sample = lax.broadcasted_iota(jnp.int32, (NT, traces), 0)
        for v in range(points):
            x = field_factor(get_point(x_scratch, v, points))
            down = jnp.where(sample < onset_ref[v : v + 1, :], dot_nn(back, x), 0.0)
            set_point(y_scratch, v, points, transform(forward, table_ref, down))
        put_pieces(y_scratch, outs, points, parts, more if extra else None)

    def transform(forward, table_ref, down):
        high, low = split(down)
        p = dot_nn(forward, high)
        return p[:rows] + p[rows:] + dot_nn(table_ref[...].astype(BF16), low)

    return pl.pallas_call(
        kernel,
        in_specs=[ON_CHIP] * (count + len(extra) + 2),
        out_specs=[ON_CHIP] * count,
        out_shape=[OUT(s) for s in shapes],
        scratch_shapes=[rows_scratch(rows * points, traces)] * 2,
        compiler_params=pltpu.CompilerParams(vmem_limit_bytes=LIMIT),
    )(*on_chip([*pieces, *extra, table, onset]))


def finish(pieces, table, onset, field, parts):
    points, traces = onset.shape
    rows = table.shape[0]
    count = len(pieces)

    def kernel(*refs):
        ins = refs[:count]
        table_ref, onset_ref, field_ref, out_ref, scratch, factor = refs[count:]
        v = pl.program_id(0)

        @pl.when(v == 0)
        def _():
            take_pieces(scratch, ins, points, parts)
            factor[...] = inverse_factor(table_ref[...]).astype(BF16)

        x = field_factor(get_point(scratch, v, points))
        g = dot_tn(x, factor[...])
        sample = lax.broadcasted_iota(jnp.int32, (traces, NT), 1)
        out_ref[0] = field_ref[0] + jnp.where(sample < onset_ref[0], g, 0.0)

    block = pl.BlockSpec((1, traces, NT), lambda v: (v, 0, 0))
    return pl.pallas_call(
        kernel,
        grid=(points,),
        in_specs=[whole(p.shape) for p in pieces]
        + [whole(table.shape), pl.BlockSpec((1, traces, 1), lambda v: (v, 0, 0)), block],
        out_specs=block,
        out_shape=jax.ShapeDtypeStruct(field.shape, F32),
        scratch_shapes=[rows_scratch(rows * points, traces), pltpu.VMEM((3 * rows, NT), BF16)],
        compiler_params=pltpu.CompilerParams(vmem_limit_bytes=LIMIT),
    )(*pieces, table, onset[:, :, None], field)


def put_rows(both, both_turned, at, lanes, piece, sign):
    half = piece.shape[0] // 2
    rows = both.shape[0] // 2
    re, im = piece[:half], piece[half:]
    turned = jnp.concatenate([-im, re] if sign > 0 else [im, -re], axis=0)
    for target, value in ((both, piece), (both_turned, turned)):
        high, low = split(value)
        target[pl.ds(at, 2 * half), lanes] = high
        target[pl.ds(pl.multiple_of(rows + at, 16), 2 * half), lanes] = low


def convolve(partners, high, low, place, offset):
    _, slots, height, traces = partners[0].shape
    quarter, line = high.shape[2:]

    def body(place_ref, a, b, c, d, high_ref, low_ref, *rest):
        outs, (both, turned, g) = rest[:4], rest[4:]
        me = place_ref[0]
        for j in range(slots):
            for i in range(4):
                lanes = pl.ds(pl.multiple_of((me ^ i) * traces, 128), traces)
                for p, ref in enumerate((a, b, c, d)):
                    put_rows(both.at[j % 2], turned.at[j % 2], p * height, lanes, ref[i, j], 1)
            at = j + offset
            g[j % 2] = three_products(dot_nt, both[j % 2], high_ref[at, 0], low_ref[at, 0]) + three_products(
                dot_nt, turned[j % 2], high_ref[at, 1], low_ref[at, 1]
            )
            for i in range(4):
                outs[i][j] = g[j % 2, pl.ds(pl.multiple_of((me ^ i) * height, 16), height), :]

    shape = jax.ShapeDtypeStruct((slots, height, quarter), F32)
    return pl.pallas_call(
        body,
        in_specs=[pl.BlockSpec(memory_space=pltpu.SMEM)] + [ON_CHIP] * 6,
        out_specs=[ON_CHIP] * 4,
        out_shape=[OUT(shape)] * 4,
        scratch_shapes=[
            pltpu.VMEM((2, 8 * height, line), BF16),
            pltpu.VMEM((2, 8 * height, line), BF16),
            pltpu.VMEM((2, 4 * height, quarter), F32),
        ],
        compiler_params=pltpu.CompilerParams(vmem_limit_bytes=LIMIT),
    )(place, *on_chip([*partners, high, low]))


def correlate(pieces, high, low, place, offset, traces):
    slots, height, quarter = pieces[0].shape
    line = high.shape[3]

    def body(place_ref, a, b, c, d, high_ref, low_ref, own, other, sibling, both, turned, h):
        me = place_ref[0]
        for j in range(slots):
            for i, ref in enumerate((a, b, c, d)):
                at = pl.multiple_of((me ^ i) * height, 16)
                put_rows(both.at[j % 2], turned.at[j % 2], at, slice(None), ref[j], -1)
            at = j + offset
            h[j % 2] = three_products(dot_nn, both[j % 2], high_ref[at, 0], low_ref[at, 0]) + three_products(
                dot_nn, turned[j % 2], high_ref[at, 1], low_ref[at, 1]
            )
            for i in range(4):
                lanes = pl.ds(pl.multiple_of((me ^ i) * traces, 128), traces)
                own[i, j] = h[j % 2, :height, lanes]
                other[i, j] = h[j % 2, height : 2 * height, lanes]
                sibling[0, i, j] = h[j % 2, 2 * height : 3 * height, lanes]
                sibling[1, i, j] = h[j % 2, 3 * height :, lanes]

    one = jax.ShapeDtypeStruct((4, slots, height, traces), F32)
    two = jax.ShapeDtypeStruct((2, 4, slots, height, traces), F32)
    return pl.pallas_call(
        body,
        in_specs=[pl.BlockSpec(memory_space=pltpu.SMEM)] + [ON_CHIP] * 6,
        out_specs=[ON_CHIP] * 3,
        out_shape=[OUT(one), OUT(one), OUT(two)],
        scratch_shapes=[
            pltpu.VMEM((2, 8 * height, quarter), BF16),
            pltpu.VMEM((2, 8 * height, quarter), BF16),
            pltpu.VMEM((2, 4 * height, line), F32),
        ],
        compiler_params=pltpu.CompilerParams(vmem_limit_bytes=LIMIT),
    )(place, *on_chip([*pieces, high, low]))


def exchange(pieces):
    out = [pieces[0]]
    for k in range(1, 4):
        out.append(lax.ppermute(pieces[k], "freq", [(f, f ^ k) for f in range(4)]))
    return out


def swap(x, axis):
    return lax.ppermute(x, axis, [(0, 1), (1, 0)])


def after(value, earlier):
    value, *earlier = lax.optimization_barrier((value, *earlier))
    return value, earlier


def local_kernels(first_field, onset, kernel, bin_owner):
    slots = kernel.shape[0]
    traces = first_field.shape[1]
    parts = [slots // PARTS + (n < slots % PARTS) for n in range(PARTS)]
    offsets = [sum(parts[:n]) for n in range(PARTS)]
    me = lax.axis_index("freq").astype(jnp.int32)
    core = lax.axis_index("vp").astype(jnp.int32)
    place = jnp.stack([me, core])
    table = tables(bin_owner, me, slots, 4)
    moves = []
    for f in range(4):
        for x in range(2):
            for c in range(2):
                source = ((2 * x + c) * 2 + (x ^ (f & 1))) * 2 + (c ^ (f >> 1))
                moves.append((source, (f * 2 + x) * 2 + c))
    onset_inner = lax.ppermute(onset, ("freq", "src", "vp"), moves)

    def part_of(pieces, n):
        return pieces[4 * n : 4 * n + 4]

    def conv_all(pieces):
        owns = [jnp.stack(exchange(part_of(pieces, n))) for n in range(PARTS)]
        out, last = [], None
        for n, own in enumerate(owns):
            other = swap(own, "src")
            sibling = swap(own, "vp")
            if last is not None:
                other, last = after(other, last)
                out[-4:] = last
            across = swap(other, "vp")
            last = convolve((own, other, sibling, across), high, low, place, offsets[n])
            out += last
        done = []
        for n in range(PARTS):
            done += exchange(out[4 * n : 4 * n + 4])
        return done

    def corr_all(pieces):
        done, last = [], None
        for n in range(PARTS):
            ready = exchange(part_of(pieces, n))
            if last is not None:
                ready[1], last = after(ready[1], last)
                done.append(corr_end(*last))
            own, other, sibling = correlate(ready, high, low, place, offsets[n], traces)
            from_sibling = swap(sibling, "vp")
            last = [own, from_sibling[0], other + from_sibling[1]]
        done.append(corr_end(*last))
        return [p for part in done for p in part]

    def corr_end(own, mine, other):
        total = own + mine + swap(other, "src")
        return exchange([total[k] for k in range(4)])

    first = spectrum(first_field, table, parts)
    high, low = load(kernel, place)
    pieces = first
    for sweep in range(ITERS):
        inner = window(conv_all(pieces), table, onset_inner, parts)
        out = corr_all(inner)
        if sweep < ITERS - 1:
            pieces = window(out, table, onset, parts, first)
    return finish(out, table, onset, first_field, parts)


def local(first_field, onset, kernel, bin_owner):
    points, traces, samples = first_field.shape
    quarter = kernel.shape[2] // lax.axis_size("vp")
    sizes = tuple(lax.axis_size(name) for name in ("freq", "src", "vp"))
    fits = sizes == (4, 2, 2) and points == 8 and samples == NT
    if fits and traces % 128 == 0 and quarter == traces and kernel.shape[3] == 4 * traces:
        return local_kernels(first_field, onset, kernel, bin_owner)
    return local_general(first_field, onset, kernel, bin_owner)


def solution(mesh):
    in_specs = (
        P(("groups", "src", "vp"), "freq", None),
        P(("groups", "src", "vp"), "freq"),
        P(("groups", "freq"), None, "src", None),
        P(),
    )
    out_specs = P(("groups", "src", "vp"), "freq", None)
    return jax.shard_map(local, mesh=mesh, in_specs=in_specs, out_specs=out_specs, check_vma=False)
```

```python
import math

import jax
import jax.numpy as jnp
from jax import lax
from jax.experimental import pallas as pl
from jax.experimental.pallas import tpu as pltpu
from jax.sharding import PartitionSpec as P

NT = 512
NF = 24
FIRST_BIN = 4
ITERS = 2
PARTS = 2
F32 = jnp.float32
BF16 = jnp.bfloat16
LIMIT = 12 << 20


highest_precision = lax.Precision.HIGHEST


def slot_tables(bin_owner, slots_here, total_slots):
    bin_index = jnp.arange(NF, dtype=jnp.int32)
    earlier = (bin_owner[:, None] == bin_owner[None, :]) & (bin_index[None, :] < bin_index[:, None])
    rank = jnp.sum(earlier.astype(jnp.int32), axis=1)
    slot_of = bin_owner * slots_here + rank
    onehot = (slot_of[:, None] == jnp.arange(total_slots, dtype=jnp.int32)[None, :]).astype(
        jnp.float32
    )
    sample = jnp.arange(NT, dtype=jnp.int32)
    phase = sample[:, None] * (FIRST_BIN + bin_index)[None, :] % NT
    angle = phase.astype(jnp.float32) * (2.0 * math.pi / NT)
    cosine = jnp.dot(jnp.cos(angle), onehot, precision=highest_precision)
    sine = jnp.dot(jnp.sin(angle), onehot, precision=highest_precision)
    scale = 2.0 / NT
    forward_table = jnp.stack([cosine, -sine], axis=2).reshape(NT, 2 * total_slots)
    inverse_table = jnp.stack([cosine.T * scale, -(sine.T * scale)], axis=1).reshape(
        2 * total_slots, NT
    )
    return (forward_table, inverse_table)


def convolve_pairs(spectrum, kernel_view):

    def product(left, right):
        return jnp.einsum("edcvr,cfsdr->efcvs", left, right, precision=highest_precision)

    real_out = product(spectrum[:, :, :, 0], kernel_view[:, 0]) - product(
        spectrum[:, :, :, 1], kernel_view[:, 1]
    )
    imag_out = product(spectrum[:, :, :, 1], kernel_view[:, 0]) + product(
        spectrum[:, :, :, 0], kernel_view[:, 1]
    )
    return jnp.stack([real_out, imag_out], axis=3)


def correlate_pairs(spectrum, kernel_view):

    def product(left, right):
        return jnp.einsum("efcvr,cfrdq->edcvq", left, right, precision=highest_precision)

    real_out = product(spectrum[:, :, :, 0], kernel_view[:, 0]) + product(
        spectrum[:, :, :, 1], kernel_view[:, 1]
    )
    imag_out = product(spectrum[:, :, :, 1], kernel_view[:, 0]) - product(
        spectrum[:, :, :, 0], kernel_view[:, 1]
    )
    return jnp.stack([real_out, imag_out], axis=3)


def local_general(first_field, onset, kernel, bin_owner):
    slots_here = kernel.shape[0]
    freq_count = lax.axis_size("freq")
    src_count = lax.axis_size("src")
    sub_blocks = freq_count // src_count
    total_slots = slots_here * freq_count
    forward_table, inverse_table = slot_tables(bin_owner, slots_here, total_slots)
    points = first_field.shape[0]
    traces = first_field.shape[1]
    kernel_view = kernel.reshape(slots_here, 2, sub_blocks, traces, freq_count, traces)
    sample = jnp.arange(NT, dtype=jnp.int32)
    keep = (sample[None, None, :] < onset[:, :, None]).astype(jnp.float32)

    def to_bins(field):
        spectrum = jnp.einsum("vrt,tc->cvr", field, forward_table, precision=highest_precision)
        spectrum = spectrum.reshape(freq_count, slots_here, 2, points, traces)
        return lax.all_to_all(spectrum, "freq", split_axis=0, concat_axis=0, tiled=True)

    def to_time(spectrum):
        regrouped = lax.all_to_all(spectrum, "freq", split_axis=0, concat_axis=0, tiled=True)
        flat = regrouped.reshape(2 * total_slots, points, traces)
        return jnp.einsum("cvr,ct->vrt", flat, inverse_table, precision=highest_precision)

    def widen(spectrum):
        return lax.all_gather(spectrum[None], "src", axis=0, tiled=True)

    focusing = first_field
    for sweep in range(ITERS):
        widened = widen(to_bins(focusing))
        direct = convolve_pairs(widened, kernel_view)
        direct = lax.all_to_all(direct, "src", split_axis=0, concat_axis=0, tiled=True)
        direct = direct.reshape(freq_count, slots_here, 2, points, traces)
        down = keep * to_time(direct)
        spectrum = to_bins(down)
        local_part = lax.dynamic_slice_in_dim(
            widen(spectrum), lax.axis_index("src") * sub_blocks, sub_blocks, 1
        )
        partial_terms = correlate_pairs(local_part, kernel_view)
        summed = lax.psum_scatter(partial_terms, "src", scatter_dimension=0, tiled=True)
        summed = summed.reshape(freq_count, slots_here, 2, points, traces)
        focusing = first_field + keep * to_time(summed)
    return focusing


def split(x):
    high = x.astype(BF16)
    return high, (x - high.astype(F32)).astype(BF16)


def stacked_split(x):
    high, low = split(x)
    return jnp.concatenate([high.astype(F32), low.astype(F32)], axis=0).astype(BF16)


def dot_nt(a, b):
    return lax.dot_general(a, b, (((1,), (1,)), ((), ())), preferred_element_type=F32)


def dot_nn(a, b):
    return lax.dot_general(a, b, (((1,), (0,)), ((), ())), preferred_element_type=F32)


def dot_tn(a, b):
    return lax.dot_general(a, b, (((0,), (0,)), ((), ())), preferred_element_type=F32)


def three_products(dot, both, high, low):
    rows = both.shape[0] // 2
    p = dot(both, high)
    return p[:rows] + p[rows:] + dot(both[:rows], low)


def tables(bin_owner, me, slots, freqs):
    owner = jnp.bitwise_xor(me, jnp.arange(freqs, dtype=jnp.int32))
    start = jnp.sum((bin_owner[None, :] < owner[:, None]).astype(jnp.int32), axis=1)
    count = jnp.sum((bin_owner[None, :] == owner[:, None]).astype(jnp.int32), axis=1)
    slot = jnp.arange(slots, dtype=jnp.int32)
    index = start[:, None] + slot[None, :] + FIRST_BIN
    valid = slot[None, :] < count[:, None]
    sample = jnp.arange(NT, dtype=jnp.int32)
    phase = index[:, :, None] * sample % NT
    angle = phase.astype(F32) * (2.0 * math.pi / NT)
    pair = jnp.stack([jnp.cos(angle), -jnp.sin(angle)], axis=2)
    return jnp.where(valid[:, :, None, None], pair, 0.0).reshape(freqs * slots * 2, NT)


def OUT(shape):
    return pltpu.VMEM(shape.shape, shape.dtype)


ON_CHIP = pl.BlockSpec(memory_space=pltpu.VMEM)


def on_chip(values):
    return [pltpu.with_memory_space_constraint(value, pltpu.VMEM) for value in values]


def load(kernel, place):
    slots, pair, sources, line = kernel.shape
    quarter = sources // 2
    shape = (pair, quarter, line)

    def body(place_ref, k, *refs):
        highs, lows, (done_ref, buffer, sems) = refs[:slots], refs[slots:-3], refs[-3:]
        done_ref[...] = jnp.zeros_like(done_ref)

        def copy(n):
            rows = pl.ds(pl.multiple_of(place_ref[1] * quarter, 8), quarter)
            source = k.at[n // pair, n % pair, rows, :]
            return pltpu.make_async_copy(source, buffer.at[n % 3], sems.at[n % 3])

        copy(0).start()
        copy(1).start()
        for n in range(slots * pair):
            if n + 2 < slots * pair:
                copy(n + 2).start()
            copy(n).wait()
            high, low = split(buffer[n % 3])
            highs[n // pair][n % pair] = high
            lows[n // pair][n % pair] = low

    *halves, loaded = pl.pallas_call(
        body,
        in_specs=[pl.BlockSpec(memory_space=pltpu.SMEM), pl.BlockSpec(memory_space=pl.ANY)],
        out_specs=[ON_CHIP] * (2 * slots + 1),
        out_shape=[pltpu.VMEM(shape, BF16)] * (2 * slots) + [pltpu.VMEM((8, 128), F32)],
        scratch_shapes=[pltpu.VMEM((3, quarter, line), F32), pltpu.SemaphoreType.DMA((3,))],
        compiler_params=pltpu.CompilerParams(vmem_limit_bytes=LIMIT),
    )(place, kernel)
    return halves[:slots], halves[slots:], loaded


def whole(shape):
    zeros = (0,) * len(shape)
    return pl.BlockSpec(shape, lambda *_: zeros)


def spectrum_kernel(points, parts, u, table, *rest):
    outs, scratch, both = rest[:-2], rest[-2], rest[-1]
    v = pl.program_id(0)

    @pl.when(v == 0)
    def _():
        both[...] = stacked_split(table[...])

    rows = table.shape[0]
    high, low = split(u[0])
    p = dot_nt(both[...], high)
    s = p[:rows] + p[rows:] + dot_nt(table[...].astype(BF16), low)
    set_point(scratch, v, points, s)

    @pl.when(v == points - 1)
    def _():
        put_pieces(scratch, outs, points, parts)


def set_point(scratch, v, points, value):
    for i in range(scratch.shape[0]):
        scratch[i, pl.ds(v, value.shape[0], stride=points), :] = value[:, 128 * i : 128 * i + 128]


def get_point(scratch, v, points):
    tiles = range(scratch.shape[0])
    rows = scratch.shape[1] // points
    return jnp.concatenate([scratch[i, pl.ds(v, rows, stride=points), :] for i in tiles], axis=1)


def rows_scratch(rows, traces):
    return pltpu.VMEM((traces // 128, rows, 128), F32)


def put_pieces(scratch, outs, points, parts, extra=None):
    height = 2 * points
    row = 0
    slots = sum(parts)
    for k in range(4):
        done = 0
        for n, size in enumerate(parts):
            for j in range(size):
                row = (k * slots + done + j) * height
                for i in range(scratch.shape[0]):
                    lanes = slice(128 * i, 128 * i + 128)
                    value = scratch[i, row : row + height, :]
                    if extra is not None:
                        value = value + extra[4 * n + k][j, :, lanes]
                    outs[4 * n + k][j, :, lanes] = value
            done += size


def take_pieces(scratch, ins, points, parts):
    height = 2 * points
    slots = sum(parts)
    for k in range(4):
        done = 0
        for n, size in enumerate(parts):
            for j in range(size):
                row = (k * slots + done + j) * height
                for i in range(scratch.shape[0]):
                    lanes = slice(128 * i, 128 * i + 128)
                    scratch[i, row : row + height, :] = ins[4 * n + k][j, :, lanes]
            done += size


def piece_shapes(parts, height, traces):
    return [jax.ShapeDtypeStruct((size, height, traces), F32) for size in parts for _ in range(4)]


def spectrum(field, table, parts):
    points, traces, _ = field.shape
    rows = table.shape[0]
    shapes = piece_shapes(parts, 2 * points, traces)

    def kernel(*refs):
        spectrum_kernel(points, parts, *refs)

    return pl.pallas_call(
        kernel,
        grid=(points,),
        in_specs=[pl.BlockSpec((1, traces, NT), lambda v: (v, 0, 0)), whole(table.shape)],
        out_specs=[whole(s.shape) for s in shapes],
        out_shape=shapes,
        scratch_shapes=[rows_scratch(rows * points, traces), pltpu.VMEM((2 * rows, NT), BF16)],
        compiler_params=pltpu.CompilerParams(vmem_limit_bytes=LIMIT),
    )(field, table)


def inverse_factor(table):
    high, low = split(table * (2.0 / NT))
    high, low = high.astype(F32), low.astype(F32)
    return jnp.concatenate([high, low, high], axis=0)


def field_factor(x):
    high, low = split(x)
    high, low = high.astype(F32), low.astype(F32)
    return jnp.concatenate([high, high, low], axis=0).astype(BF16)


def window(pieces, table, onset, parts, parts_out, extra=None):
    points, traces = onset.shape
    rows = table.shape[0]
    shapes = piece_shapes(parts_out, 2 * points, traces)
    count = len(pieces)
    extra = list(extra) if extra is not None else []

    def kernel(*refs):
        ins, refs = refs[:count], refs[count:]
        more, refs = refs[: len(extra)], refs[len(extra) :]
        table_ref, onset_ref = refs[:2]
        outs, (x_scratch, y_scratch) = refs[2:-2], refs[-2:]
        take_pieces(x_scratch, ins, points, parts)
        forward = stacked_split(table_ref[...])
        back = inverse_factor(table_ref[...]).T.astype(BF16)
        sample = lax.broadcasted_iota(jnp.int32, (NT, traces), 0)
        for v in range(points):
            x = field_factor(get_point(x_scratch, v, points))
            down = jnp.where(sample < onset_ref[v : v + 1, :], dot_nn(back, x), 0.0)
            set_point(y_scratch, v, points, transform(forward, table_ref, down))
        put_pieces(y_scratch, outs, points, parts_out, more if extra else None)

    def transform(forward, table_ref, down):
        high, low = split(down)
        p = dot_nn(forward, high)
        return p[:rows] + p[rows:] + dot_nn(table_ref[...].astype(BF16), low)

    return pl.pallas_call(
        kernel,
        in_specs=[ON_CHIP] * (count + len(extra) + 2),
        out_specs=[ON_CHIP] * len(shapes),
        out_shape=[OUT(s) for s in shapes],
        scratch_shapes=[rows_scratch(rows * points, traces)] * 2,
        compiler_params=pltpu.CompilerParams(vmem_limit_bytes=LIMIT),
    )(*on_chip([*pieces, *extra, table, onset]))


def finish(pieces, table, onset, field, parts):
    points, traces = onset.shape
    rows = table.shape[0]
    count = len(pieces)

    def kernel(*refs):
        ins = refs[:count]
        table_ref, onset_ref, field_ref, out_ref, scratch, factor = refs[count:]
        v = pl.program_id(0)

        @pl.when(v == 0)
        def _():
            take_pieces(scratch, ins, points, parts)
            factor[...] = inverse_factor(table_ref[...]).astype(BF16)

        x = field_factor(get_point(scratch, v, points))
        g = dot_tn(x, factor[...])
        sample = lax.broadcasted_iota(jnp.int32, (traces, NT), 1)
        out_ref[0] = field_ref[0] + jnp.where(sample < onset_ref[0], g, 0.0)

    block = pl.BlockSpec((1, traces, NT), lambda v: (v, 0, 0))
    return pl.pallas_call(
        kernel,
        grid=(points,),
        in_specs=[whole(p.shape) for p in pieces]
        + [whole(table.shape), pl.BlockSpec((1, traces, 1), lambda v: (v, 0, 0)), block],
        out_specs=block,
        out_shape=jax.ShapeDtypeStruct(field.shape, F32),
        scratch_shapes=[rows_scratch(rows * points, traces), pltpu.VMEM((3 * rows, NT), BF16)],
        compiler_params=pltpu.CompilerParams(vmem_limit_bytes=LIMIT),
    )(*pieces, table, onset[:, :, None], field)


def put_rows(both, both_turned, at, lanes, piece, sign):
    half = piece.shape[0] // 2
    rows = both.shape[0] // 2
    re, im = piece[:half], piece[half:]
    turned = jnp.concatenate([-im, re] if sign > 0 else [im, -re], axis=0)
    for target, value in ((both, piece), (both_turned, turned)):
        high, low = split(value)
        target[pl.ds(at, 2 * half), lanes] = high
        target[pl.ds(pl.multiple_of(rows + at, 16), 2 * half), lanes] = low


def convolve(partners, high, low, place):
    _, slots, height, traces = partners[0].shape
    quarter, line = high[0].shape[1:]

    def body(place_ref, a, b, c, d, *rest):
        highs, lows, rest = rest[:slots], rest[slots : 2 * slots], rest[2 * slots :]
        outs, (both, turned, g) = rest[:4], rest[4:]
        me = place_ref[0]
        for j in range(slots):
            for i in range(4):
                lanes = pl.ds(pl.multiple_of((me ^ i) * traces, 128), traces)
                for p, ref in enumerate((a, b, c, d)):
                    put_rows(both.at[j % 2], turned.at[j % 2], p * height, lanes, ref[i, j], 1)
            g[j % 2] = three_products(dot_nt, both[j % 2], highs[j][0], lows[j][0]) + three_products(
                dot_nt, turned[j % 2], highs[j][1], lows[j][1]
            )
            for i in range(4):
                outs[i][j] = g[j % 2, pl.ds(pl.multiple_of((me ^ i) * height, 16), height), :]

    shape = jax.ShapeDtypeStruct((slots, height, quarter), F32)
    return pl.pallas_call(
        body,
        in_specs=[pl.BlockSpec(memory_space=pltpu.SMEM)] + [ON_CHIP] * (4 + 2 * slots),
        out_specs=[ON_CHIP] * 4,
        out_shape=[OUT(shape)] * 4,
        scratch_shapes=[
            pltpu.VMEM((2, 8 * height, line), BF16),
            pltpu.VMEM((2, 8 * height, line), BF16),
            pltpu.VMEM((2, 4 * height, quarter), F32),
        ],
        compiler_params=pltpu.CompilerParams(vmem_limit_bytes=LIMIT),
    )(place, *on_chip([*partners, *high, *low]))


def correlate(pieces, high, low, place, offset, traces):
    slots = len(high)
    _, height, quarter = pieces[0].shape
    line = high[0].shape[2]

    def body(place_ref, a, b, c, d, *rest):
        highs, lows, rest = rest[:slots], rest[slots : 2 * slots], rest[2 * slots :]
        own, other, sibling, both, turned, h = rest
        me = place_ref[0]
        for j in range(slots):
            for i, ref in enumerate((a, b, c, d)):
                at = pl.multiple_of((me ^ i) * height, 16)
                put_rows(both.at[j % 2], turned.at[j % 2], at, slice(None), ref[j + offset], -1)
            h[j % 2] = three_products(dot_nn, both[j % 2], highs[j][0], lows[j][0]) + three_products(
                dot_nn, turned[j % 2], highs[j][1], lows[j][1]
            )
            for i in range(4):
                lanes = pl.ds(pl.multiple_of((me ^ i) * traces, 128), traces)
                own[i, j] = h[j % 2, :height, lanes]
                other[i, j] = h[j % 2, height : 2 * height, lanes]
                sibling[0, i, j] = h[j % 2, 2 * height : 3 * height, lanes]
                sibling[1, i, j] = h[j % 2, 3 * height :, lanes]

    one = jax.ShapeDtypeStruct((4, slots, height, traces), F32)
    two = jax.ShapeDtypeStruct((2, 4, slots, height, traces), F32)
    return pl.pallas_call(
        body,
        in_specs=[pl.BlockSpec(memory_space=pltpu.SMEM)] + [ON_CHIP] * (4 + 2 * slots),
        out_specs=[ON_CHIP] * 3,
        out_shape=[OUT(one), OUT(one), OUT(two)],
        scratch_shapes=[
            pltpu.VMEM((2, 8 * height, quarter), BF16),
            pltpu.VMEM((2, 8 * height, quarter), BF16),
            pltpu.VMEM((2, 4 * height, line), F32),
        ],
        compiler_params=pltpu.CompilerParams(vmem_limit_bytes=LIMIT),
    )(place, *on_chip([*pieces, *high, *low]))


def exchange(pieces):
    out = [pieces[0]]
    for k in range(1, 4):
        out.append(lax.ppermute(pieces[k], "freq", [(f, f ^ k) for f in range(4)]))
    return out


def swap(x, axis):
    return lax.ppermute(x, axis, [(0, 1), (1, 0)])


def after(value, earlier):
    value, *earlier = lax.optimization_barrier((value, *earlier))
    return value, earlier


def local_kernels(first_field, onset, kernel, bin_owner):
    slots = kernel.shape[0]
    traces = first_field.shape[1]
    parts = [slots // PARTS + (n < slots % PARTS) for n in range(PARTS)]
    offsets = [sum(parts[:n]) for n in range(PARTS)]
    me = lax.axis_index("freq").astype(jnp.int32)
    core = lax.axis_index("vp").astype(jnp.int32)
    place = jnp.stack([me, core])
    table = tables(bin_owner, me, slots, 4)
    moves = []
    for f in range(4):
        for x in range(2):
            for c in range(2):
                source = ((2 * x + c) * 2 + (x ^ (f & 1))) * 2 + (c ^ (f >> 1))
                moves.append((source, (f * 2 + x) * 2 + c))
    onset_inner = lax.ppermute(onset, ("freq", "src", "vp"), moves)

    def part_of(pieces, n):
        return pieces[4 * n : 4 * n + 4]

    def kernel_part(n):
        part = slice(offsets[n], offsets[n] + parts[n])
        return high[part], low[part]

    def conv_all(pieces, loaded):
        owns = []
        for n in range(PARTS):
            ready = exchange(part_of(pieces, n))
            if loaded is not None:
                ready[1], _ = after(ready[1], [loaded])
            owns.append(jnp.stack(ready))
        out, last = [], None
        for n, own in enumerate(owns):
            other = swap(own, "src")
            sibling = swap(own, "vp")
            if last is not None:
                other, last = after(other, last)
                out[-4:] = last
            across = swap(other, "vp")
            last = convolve((own, other, sibling, across), *kernel_part(n), place)
            out += last
        done = []
        for n in range(PARTS):
            done += exchange(out[4 * n : 4 * n + 4])
        return done

    def corr_all(pieces):
        ready = exchange(pieces)
        sums, turn = [], place
        for n in range(PARTS):
            own, other, sibling = correlate(ready, *kernel_part(n), turn, offsets[n], traces)
            from_sibling = swap(sibling, "vp")
            other = other + from_sibling[1]
            turn, (other,) = after(turn, [other])
            sums.append((own, from_sibling[0], swap(other, "src")))
        done = []
        for own, mine, other in sums:
            total = own + mine + other
            done += exchange([total[k] for k in range(4)])
        return done

    first = spectrum(first_field, table, parts)
    high, low, loaded = load(kernel, place)
    pieces = first
    for sweep in range(ITERS):
        out = conv_all(pieces, loaded if sweep == 0 else None)
        out = corr_all(window(out, table, onset_inner, parts, [slots]))
        if sweep < ITERS - 1:
            pieces = window(out, table, onset, parts, parts, first)
    return finish(out, table, onset, first_field, parts)


def local(first_field, onset, kernel, bin_owner):
    points, traces, samples = first_field.shape
    quarter = kernel.shape[2] // lax.axis_size("vp")
    sizes = tuple(lax.axis_size(name) for name in ("freq", "src", "vp"))
    fits = sizes == (4, 2, 2) and points == 8 and samples == NT
    if fits and traces % 128 == 0 and quarter == traces and kernel.shape[3] == 4 * traces:
        return local_kernels(first_field, onset, kernel, bin_owner)
    return local_general(first_field, onset, kernel, bin_owner)


def solution(mesh):
    in_specs = (
        P(("groups", "src", "vp"), "freq", None),
        P(("groups", "src", "vp"), "freq"),
        P(("groups", "freq"), None, "src", None),
        P(),
    )
    out_specs = P(("groups", "src", "vp"), "freq", None)
    return jax.shard_map(local, mesh=mesh, in_specs=in_specs, out_specs=out_specs, check_vma=False)
```

```python
import math

import jax
import jax.numpy as jnp
from jax import lax
from jax.experimental import pallas as pl
from jax.experimental.pallas import tpu as pltpu
from jax.sharding import PartitionSpec as P

NT = 512
NF = 24
FIRST_BIN = 4
ITERS = 2
PARTS = 2
F32 = jnp.float32
BF16 = jnp.bfloat16
LIMIT = 12 << 20


highest_precision = lax.Precision.HIGHEST


def slot_tables(bin_owner, slots_here, total_slots):
    bin_index = jnp.arange(NF, dtype=jnp.int32)
    earlier = (bin_owner[:, None] == bin_owner[None, :]) & (bin_index[None, :] < bin_index[:, None])
    rank = jnp.sum(earlier.astype(jnp.int32), axis=1)
    slot_of = bin_owner * slots_here + rank
    onehot = (slot_of[:, None] == jnp.arange(total_slots, dtype=jnp.int32)[None, :]).astype(
        jnp.float32
    )
    sample = jnp.arange(NT, dtype=jnp.int32)
    phase = sample[:, None] * (FIRST_BIN + bin_index)[None, :] % NT
    angle = phase.astype(jnp.float32) * (2.0 * math.pi / NT)
    cosine = jnp.dot(jnp.cos(angle), onehot, precision=highest_precision)
    sine = jnp.dot(jnp.sin(angle), onehot, precision=highest_precision)
    scale = 2.0 / NT
    forward_table = jnp.stack([cosine, -sine], axis=2).reshape(NT, 2 * total_slots)
    inverse_table = jnp.stack([cosine.T * scale, -(sine.T * scale)], axis=1).reshape(
        2 * total_slots, NT
    )
    return (forward_table, inverse_table)


def convolve_pairs(spectrum, kernel_view):

    def product(left, right):
        return jnp.einsum("edcvr,cfsdr->efcvs", left, right, precision=highest_precision)

    real_out = product(spectrum[:, :, :, 0], kernel_view[:, 0]) - product(
        spectrum[:, :, :, 1], kernel_view[:, 1]
    )
    imag_out = product(spectrum[:, :, :, 1], kernel_view[:, 0]) + product(
        spectrum[:, :, :, 0], kernel_view[:, 1]
    )
    return jnp.stack([real_out, imag_out], axis=3)


def correlate_pairs(spectrum, kernel_view):

    def product(left, right):
        return jnp.einsum("efcvr,cfrdq->edcvq", left, right, precision=highest_precision)

    real_out = product(spectrum[:, :, :, 0], kernel_view[:, 0]) + product(
        spectrum[:, :, :, 1], kernel_view[:, 1]
    )
    imag_out = product(spectrum[:, :, :, 1], kernel_view[:, 0]) - product(
        spectrum[:, :, :, 0], kernel_view[:, 1]
    )
    return jnp.stack([real_out, imag_out], axis=3)


def local_general(first_field, onset, kernel, bin_owner):
    slots_here = kernel.shape[0]
    freq_count = lax.axis_size("freq")
    src_count = lax.axis_size("src")
    sub_blocks = freq_count // src_count
    total_slots = slots_here * freq_count
    forward_table, inverse_table = slot_tables(bin_owner, slots_here, total_slots)
    points = first_field.shape[0]
    traces = first_field.shape[1]
    kernel_view = kernel.reshape(slots_here, 2, sub_blocks, traces, freq_count, traces)
    sample = jnp.arange(NT, dtype=jnp.int32)
    keep = (sample[None, None, :] < onset[:, :, None]).astype(jnp.float32)

    def to_bins(field):
        spectrum = jnp.einsum("vrt,tc->cvr", field, forward_table, precision=highest_precision)
        spectrum = spectrum.reshape(freq_count, slots_here, 2, points, traces)
        return lax.all_to_all(spectrum, "freq", split_axis=0, concat_axis=0, tiled=True)

    def to_time(spectrum):
        regrouped = lax.all_to_all(spectrum, "freq", split_axis=0, concat_axis=0, tiled=True)
        flat = regrouped.reshape(2 * total_slots, points, traces)
        return jnp.einsum("cvr,ct->vrt", flat, inverse_table, precision=highest_precision)

    def widen(spectrum):
        return lax.all_gather(spectrum[None], "src", axis=0, tiled=True)

    focusing = first_field
    for sweep in range(ITERS):
        widened = widen(to_bins(focusing))
        direct = convolve_pairs(widened, kernel_view)
        direct = lax.all_to_all(direct, "src", split_axis=0, concat_axis=0, tiled=True)
        direct = direct.reshape(freq_count, slots_here, 2, points, traces)
        down = keep * to_time(direct)
        spectrum = to_bins(down)
        local_part = lax.dynamic_slice_in_dim(
            widen(spectrum), lax.axis_index("src") * sub_blocks, sub_blocks, 1
        )
        partial_terms = correlate_pairs(local_part, kernel_view)
        summed = lax.psum_scatter(partial_terms, "src", scatter_dimension=0, tiled=True)
        summed = summed.reshape(freq_count, slots_here, 2, points, traces)
        focusing = first_field + keep * to_time(summed)
    return focusing


def split(x):
    high = x.astype(BF16)
    return high, (x - high.astype(F32)).astype(BF16)


def stacked_split(x):
    high, low = split(x)
    return jnp.concatenate([high.astype(F32), low.astype(F32)], axis=0).astype(BF16)


def dot_nt(a, b):
    return lax.dot_general(a, b, (((1,), (1,)), ((), ())), preferred_element_type=F32)


def dot_nn(a, b):
    return lax.dot_general(a, b, (((1,), (0,)), ((), ())), preferred_element_type=F32)


def dot_tn(a, b):
    return lax.dot_general(a, b, (((0,), (0,)), ((), ())), preferred_element_type=F32)


def three_products(dot, both, high, low):
    rows = both.shape[0] // 2
    p = dot(both, high)
    return p[:rows] + p[rows:] + dot(both[:rows], low)


def tables(bin_owner, me, slots, freqs):
    owner = jnp.bitwise_xor(me, jnp.arange(freqs, dtype=jnp.int32))
    start = jnp.sum((bin_owner[None, :] < owner[:, None]).astype(jnp.int32), axis=1)
    count = jnp.sum((bin_owner[None, :] == owner[:, None]).astype(jnp.int32), axis=1)
    slot = jnp.arange(slots, dtype=jnp.int32)
    index = start[:, None] + slot[None, :] + FIRST_BIN
    valid = slot[None, :] < count[:, None]
    sample = jnp.arange(NT, dtype=jnp.int32)
    phase = index[:, :, None] * sample % NT
    angle = phase.astype(F32) * (2.0 * math.pi / NT)
    pair = jnp.stack([jnp.cos(angle), -jnp.sin(angle)], axis=2)
    return jnp.where(valid[:, :, None, None], pair, 0.0).reshape(freqs * slots * 2, NT)


def OUT(shape):
    return pltpu.VMEM(shape.shape, shape.dtype)


ON_CHIP = pl.BlockSpec(memory_space=pltpu.VMEM)


def on_chip(values):
    return [pltpu.with_memory_space_constraint(value, pltpu.VMEM) for value in values]


def load(kernel, place):
    slots, pair, sources, line = kernel.shape
    quarter = sources // 2
    shape = (pair, quarter, line)

    def body(place_ref, k, *refs):
        highs, lows, (done_ref, buffer, sems) = refs[:slots], refs[slots:-3], refs[-3:]
        done_ref[...] = jnp.zeros_like(done_ref)

        def copy(n):
            rows = pl.ds(pl.multiple_of(place_ref[1] * quarter, 8), quarter)
            source = k.at[n // pair, n % pair, rows, :]
            return pltpu.make_async_copy(source, buffer.at[n % 3], sems.at[n % 3])

        copy(0).start()
        copy(1).start()
        for n in range(slots * pair):
            if n + 2 < slots * pair:
                copy(n + 2).start()
            copy(n).wait()
            high, low = split(buffer[n % 3])
            highs[n // pair][n % pair] = high
            lows[n // pair][n % pair] = low

    *halves, loaded = pl.pallas_call(
        body,
        in_specs=[pl.BlockSpec(memory_space=pltpu.SMEM), pl.BlockSpec(memory_space=pl.ANY)],
        out_specs=[ON_CHIP] * (2 * slots + 1),
        out_shape=[pltpu.VMEM(shape, BF16)] * (2 * slots) + [pltpu.VMEM((8, 128), F32)],
        scratch_shapes=[pltpu.VMEM((3, quarter, line), F32), pltpu.SemaphoreType.DMA((3,))],
        compiler_params=pltpu.CompilerParams(vmem_limit_bytes=LIMIT),
    )(place, kernel)
    return halves[:slots], halves[slots:], loaded


def whole(shape):
    zeros = (0,) * len(shape)
    return pl.BlockSpec(shape, lambda *_: zeros)


def field_copy(source, field, sems, v):
    return pltpu.make_async_copy(source.at[v], field.at[v], sems.at[v])


def spectrum_kernel(points, parts, source, table, *rest):
    outs, (scratch, both, field, sems) = rest[:-4], rest[-4:]
    v = pl.program_id(0)

    @pl.when(v == 0)
    def _():
        for p in range(points):
            field_copy(source, field, sems, p).start()
        both[...] = stacked_split(table[...])

    rows = table.shape[0]
    field_copy(source, field, sems, v).wait()
    high, low = split(field[v])
    p = dot_nt(both[...], high)
    s = p[:rows] + p[rows:] + dot_nt(table[...].astype(BF16), low)
    set_point(scratch, v, points, s)

    @pl.when(v == points - 1)
    def _():
        put_pieces(scratch, outs, points, parts)


def set_point(scratch, v, points, value):
    for i in range(scratch.shape[0]):
        scratch[i, pl.ds(v, value.shape[0], stride=points), :] = value[:, 128 * i : 128 * i + 128]


def get_point(scratch, v, points):
    tiles = range(scratch.shape[0])
    rows = scratch.shape[1] // points
    return jnp.concatenate([scratch[i, pl.ds(v, rows, stride=points), :] for i in tiles], axis=1)


def rows_scratch(rows, traces):
    return pltpu.VMEM((traces // 128, rows, 128), F32)


def put_pieces(scratch, outs, points, parts, extra=None):
    height = 2 * points
    row = 0
    slots = sum(parts)
    for k in range(4):
        done = 0
        for n, size in enumerate(parts):
            for j in range(size):
                row = (k * slots + done + j) * height
                for i in range(scratch.shape[0]):
                    lanes = slice(128 * i, 128 * i + 128)
                    value = scratch[i, row : row + height, :]
                    if extra is not None:
                        value = value + extra[k][done + j, :, lanes]
                    outs[4 * n + k][j, :, lanes] = value
            done += size


def take_pieces(scratch, ins, points, parts):
    height = 2 * points
    slots = sum(parts)
    for k in range(4):
        done = 0
        for n, size in enumerate(parts):
            for j in range(size):
                row = (k * slots + done + j) * height
                for i in range(scratch.shape[0]):
                    lanes = slice(128 * i, 128 * i + 128)
                    scratch[i, row : row + height, :] = ins[4 * n + k][j, :, lanes]
            done += size


def piece_shapes(parts, height, traces):
    return [jax.ShapeDtypeStruct((size, height, traces), F32) for size in parts for _ in range(4)]


def field_scratch(field):
    return [pltpu.VMEM(field.shape, F32), pltpu.SemaphoreType.DMA((field.shape[0],))]


def spectrum(field, table, parts):
    points, traces, _ = field.shape
    rows = table.shape[0]
    shapes = piece_shapes(parts, 2 * points, traces)

    def kernel(*refs):
        spectrum_kernel(points, parts, *refs)

    return pl.pallas_call(
        kernel,
        grid=(points,),
        in_specs=[pl.BlockSpec(memory_space=pl.ANY), whole(table.shape)],
        out_specs=[whole(s.shape) for s in shapes],
        out_shape=shapes,
        scratch_shapes=[rows_scratch(rows * points, traces), pltpu.VMEM((2 * rows, NT), BF16)]
        + field_scratch(field),
        compiler_params=pltpu.CompilerParams(vmem_limit_bytes=LIMIT),
    )(pltpu.with_memory_space_constraint(field, pltpu.HBM), table)


def inverse_factor(table):
    high, low = split(table * (2.0 / NT))
    high, low = high.astype(F32), low.astype(F32)
    return jnp.concatenate([high, low, high], axis=0)


def field_factor(x):
    high, low = split(x)
    high, low = high.astype(F32), low.astype(F32)
    return jnp.concatenate([high, high, low], axis=0).astype(BF16)


def window(pieces, table, onset, parts, parts_out, extra=None):
    points, traces = onset.shape
    rows = table.shape[0]
    shapes = piece_shapes(parts_out, 2 * points, traces)
    count = len(pieces)
    extra = list(extra) if extra is not None else []

    def kernel(*refs):
        ins, refs = refs[:count], refs[count:]
        more, refs = refs[: len(extra)], refs[len(extra) :]
        table_ref, onset_ref = refs[:2]
        outs, (x_scratch, y_scratch) = refs[2:-2], refs[-2:]
        take_pieces(x_scratch, ins, points, parts)
        forward = stacked_split(table_ref[...])
        back = inverse_factor(table_ref[...]).T.astype(BF16)
        sample = lax.broadcasted_iota(jnp.int32, (NT, traces), 0)
        for v in range(points):
            x = field_factor(get_point(x_scratch, v, points))
            down = jnp.where(sample < onset_ref[v : v + 1, :], dot_nn(back, x), 0.0)
            set_point(y_scratch, v, points, transform(forward, table_ref, down))
        put_pieces(y_scratch, outs, points, parts_out, more if extra else None)

    def transform(forward, table_ref, down):
        high, low = split(down)
        p = dot_nn(forward, high)
        return p[:rows] + p[rows:] + dot_nn(table_ref[...].astype(BF16), low)

    return pl.pallas_call(
        kernel,
        in_specs=[ON_CHIP] * (count + len(extra) + 2),
        out_specs=[ON_CHIP] * len(shapes),
        out_shape=[OUT(s) for s in shapes],
        scratch_shapes=[rows_scratch(rows * points, traces)] * 2,
        compiler_params=pltpu.CompilerParams(vmem_limit_bytes=LIMIT),
    )(*on_chip([*pieces, *extra, table, onset]))


def finish(pieces, table, onset, field, parts):
    points, traces = onset.shape
    rows = table.shape[0]
    count = len(pieces)

    def kernel(*refs):
        ins = refs[:count]
        table_ref, onset_ref, source, out_ref, scratch, factor, held, sems = refs[count:]
        v = pl.program_id(0)

        @pl.when(v == 0)
        def _():
            for p in range(points):
                field_copy(source, held, sems, p).start()
            take_pieces(scratch, ins, points, parts)
            factor[...] = inverse_factor(table_ref[...]).astype(BF16)

        x = field_factor(get_point(scratch, v, points))
        g = dot_tn(x, factor[...])
        sample = lax.broadcasted_iota(jnp.int32, (traces, NT), 1)
        field_copy(source, held, sems, v).wait()
        out_ref[0] = held[v] + jnp.where(sample < onset_ref[0], g, 0.0)

    block = pl.BlockSpec((1, traces, NT), lambda v: (v, 0, 0))
    return pl.pallas_call(
        kernel,
        grid=(points,),
        in_specs=[whole(p.shape) for p in pieces]
        + [whole(table.shape), pl.BlockSpec((1, traces, 1), lambda v: (v, 0, 0)), pl.BlockSpec(memory_space=pl.ANY)],
        out_specs=block,
        out_shape=jax.ShapeDtypeStruct(field.shape, F32),
        scratch_shapes=[rows_scratch(rows * points, traces), pltpu.VMEM((3 * rows, NT), BF16)]
        + field_scratch(field),
        compiler_params=pltpu.CompilerParams(vmem_limit_bytes=LIMIT),
    )(*pieces, table, onset[:, :, None], pltpu.with_memory_space_constraint(field, pltpu.HBM))


def put_rows(both, both_turned, at, lanes, piece, sign):
    half = piece.shape[0] // 2
    rows = both.shape[0] // 2
    re, im = piece[:half], piece[half:]
    turned = jnp.concatenate([-im, re] if sign > 0 else [im, -re], axis=0)
    for target, value in ((both, piece), (both_turned, turned)):
        high, low = split(value)
        target[pl.ds(at, 2 * half), lanes] = high
        target[pl.ds(pl.multiple_of(rows + at, 16), 2 * half), lanes] = low


def convolve(partners, high, low, place):
    _, slots, height, traces = partners[0].shape
    quarter, line = high[0].shape[1:]

    def body(place_ref, a, b, c, d, *rest):
        highs, lows, rest = rest[:slots], rest[slots : 2 * slots], rest[2 * slots :]
        outs, (both, turned, g) = rest[:4], rest[4:]
        me = place_ref[0]
        for j in range(slots):
            for i in range(4):
                lanes = pl.ds(pl.multiple_of((me ^ i) * traces, 128), traces)
                for p, ref in enumerate((a, b, c, d)):
                    put_rows(both.at[j % 2], turned.at[j % 2], p * height, lanes, ref[i, j], 1)
            g[j % 2] = three_products(dot_nt, both[j % 2], highs[j][0], lows[j][0]) + three_products(
                dot_nt, turned[j % 2], highs[j][1], lows[j][1]
            )
            for i in range(4):
                outs[i][j] = g[j % 2, pl.ds(pl.multiple_of((me ^ i) * height, 16), height), :]

    shape = jax.ShapeDtypeStruct((slots, height, quarter), F32)
    return pl.pallas_call(
        body,
        in_specs=[pl.BlockSpec(memory_space=pltpu.SMEM)] + [ON_CHIP] * (4 + 2 * slots),
        out_specs=[ON_CHIP] * 4,
        out_shape=[OUT(shape)] * 4,
        scratch_shapes=[
            pltpu.VMEM((2, 8 * height, line), BF16),
            pltpu.VMEM((2, 8 * height, line), BF16),
            pltpu.VMEM((2, 4 * height, quarter), F32),
        ],
        compiler_params=pltpu.CompilerParams(vmem_limit_bytes=LIMIT),
    )(place, *on_chip([*partners, *high, *low]))


def correlate(pieces, high, low, place, offset, traces):
    slots = len(high)
    _, height, quarter = pieces[0].shape
    line = high[0].shape[2]

    def body(place_ref, a, b, c, d, *rest):
        highs, lows, rest = rest[:slots], rest[slots : 2 * slots], rest[2 * slots :]
        own, other, sibling, both, turned, h = rest
        me = place_ref[0]
        for j in range(slots):
            for i, ref in enumerate((a, b, c, d)):
                at = pl.multiple_of((me ^ i) * height, 16)
                put_rows(both.at[j % 2], turned.at[j % 2], at, slice(None), ref[j + offset], -1)
            h[j % 2] = three_products(dot_nn, both[j % 2], highs[j][0], lows[j][0]) + three_products(
                dot_nn, turned[j % 2], highs[j][1], lows[j][1]
            )
            for i in range(4):
                lanes = pl.ds(pl.multiple_of((me ^ i) * traces, 128), traces)
                own[i, j] = h[j % 2, :height, lanes]
                other[i, j] = h[j % 2, height : 2 * height, lanes]
                sibling[0, i, j] = h[j % 2, 2 * height : 3 * height, lanes]
                sibling[1, i, j] = h[j % 2, 3 * height :, lanes]

    one = jax.ShapeDtypeStruct((4, slots, height, traces), F32)
    two = jax.ShapeDtypeStruct((2, 4, slots, height, traces), F32)
    return pl.pallas_call(
        body,
        in_specs=[pl.BlockSpec(memory_space=pltpu.SMEM)] + [ON_CHIP] * (4 + 2 * slots),
        out_specs=[ON_CHIP] * 3,
        out_shape=[OUT(one), OUT(one), OUT(two)],
        scratch_shapes=[
            pltpu.VMEM((2, 8 * height, quarter), BF16),
            pltpu.VMEM((2, 8 * height, quarter), BF16),
            pltpu.VMEM((2, 4 * height, line), F32),
        ],
        compiler_params=pltpu.CompilerParams(vmem_limit_bytes=LIMIT),
    )(place, *on_chip([*pieces, *high, *low]))


def exchange(pieces):
    out = [pieces[0]]
    for k in range(1, 4):
        out.append(lax.ppermute(pieces[k], "freq", [(f, f ^ k) for f in range(4)]))
    return out


def swap(x, axis):
    return lax.ppermute(x, axis, [(0, 1), (1, 0)])


def after(value, earlier):
    value, *earlier = lax.optimization_barrier((value, *earlier))
    return value, earlier


def local_kernels(first_field, onset, kernel, bin_owner):
    slots = kernel.shape[0]
    traces = first_field.shape[1]
    parts = [slots // PARTS + (n < slots % PARTS) for n in range(PARTS)]
    offsets = [sum(parts[:n]) for n in range(PARTS)]
    me = lax.axis_index("freq").astype(jnp.int32)
    core = lax.axis_index("vp").astype(jnp.int32)
    place = jnp.stack([me, core])
    table = tables(bin_owner, me, slots, 4)
    moves = []
    for f in range(4):
        for x in range(2):
            for c in range(2):
                source = ((2 * x + c) * 2 + (x ^ (f & 1))) * 2 + (c ^ (f >> 1))
                moves.append((source, (f * 2 + x) * 2 + c))
    onset_inner = lax.ppermute(onset, ("freq", "src", "vp"), moves)

    def part_of(pieces, n):
        return pieces[4 * n : 4 * n + 4]

    def kernel_part(n):
        part = slice(offsets[n], offsets[n] + parts[n])
        return high[part], low[part]

    def conv_all(pieces, loaded):
        owns = []
        if loaded is not None:
            ready = exchange(pieces)
            for start, size in zip(offsets, parts):
                part = [piece[start : start + size] for piece in ready]
                part[1], _ = after(part[1], [loaded])
                owns.append(jnp.stack(part))
        else:
            for n in range(PARTS):
                owns.append(jnp.stack(exchange(part_of(pieces, n))))
        out, last = [], None
        for n, own in enumerate(owns):
            other = swap(own, "src")
            sibling = swap(own, "vp")
            if last is not None:
                other, last = after(other, last)
                out[-4:] = last
            across = swap(other, "vp")
            last = convolve((own, other, sibling, across), *kernel_part(n), place)
            out += last
        done = []
        for n in range(PARTS):
            done += exchange(out[4 * n : 4 * n + 4])
        return done

    def corr_all(pieces):
        ready = exchange(pieces)
        sums, turn = [], place
        for n in range(PARTS):
            own, other, sibling = correlate(ready, *kernel_part(n), turn, offsets[n], traces)
            from_sibling = swap(sibling, "vp")
            other = other + from_sibling[1]
            turn, (other,) = after(turn, [other])
            sums.append((own, from_sibling[0], swap(other, "src")))
        done = []
        for own, mine, other in sums:
            total = own + mine + other
            done += exchange([total[k] for k in range(4)])
        return done

    first = spectrum(first_field, table, [slots])
    high, low, loaded = load(kernel, place)
    pieces = first
    for sweep in range(ITERS):
        out = conv_all(pieces, loaded if sweep == 0 else None)
        out = corr_all(window(out, table, onset_inner, parts, [slots]))
        if sweep < ITERS - 1:
            pieces = window(out, table, onset, parts, parts, first)
    return finish(out, table, onset, first_field, parts)


def local(first_field, onset, kernel, bin_owner):
    points, traces, samples = first_field.shape
    quarter = kernel.shape[2] // lax.axis_size("vp")
    sizes = tuple(lax.axis_size(name) for name in ("freq", "src", "vp"))
    fits = sizes == (4, 2, 2) and points == 8 and samples == NT
    if fits and traces % 128 == 0 and quarter == traces and kernel.shape[3] == 4 * traces:
        return local_kernels(first_field, onset, kernel, bin_owner)
    return local_general(first_field, onset, kernel, bin_owner)


def solution(mesh):
    in_specs = (
        P(("groups", "src", "vp"), "freq", None),
        P(("groups", "src", "vp"), "freq"),
        P(("groups", "freq"), None, "src", None),
        P(),
    )
    out_specs = P(("groups", "src", "vp"), "freq", None)
    return jax.shard_map(local, mesh=mesh, in_specs=in_specs, out_specs=out_specs, check_vma=False)
```

```python
import math

import jax
import jax.numpy as jnp
from jax import lax
from jax.experimental import pallas as pl
from jax.experimental.pallas import tpu as pltpu
from jax.sharding import PartitionSpec as P

NT = 512
NF = 24
FIRST_BIN = 4
ITERS = 2
PARTS = 2
F32 = jnp.float32
BF16 = jnp.bfloat16
LIMIT = 12 << 20


highest_precision = lax.Precision.HIGHEST


def slot_tables(bin_owner, slots_here, total_slots):
    bin_index = jnp.arange(NF, dtype=jnp.int32)
    earlier = (bin_owner[:, None] == bin_owner[None, :]) & (bin_index[None, :] < bin_index[:, None])
    rank = jnp.sum(earlier.astype(jnp.int32), axis=1)
    slot_of = bin_owner * slots_here + rank
    onehot = (slot_of[:, None] == jnp.arange(total_slots, dtype=jnp.int32)[None, :]).astype(
        jnp.float32
    )
    sample = jnp.arange(NT, dtype=jnp.int32)
    phase = sample[:, None] * (FIRST_BIN + bin_index)[None, :] % NT
    angle = phase.astype(jnp.float32) * (2.0 * math.pi / NT)
    cosine = jnp.dot(jnp.cos(angle), onehot, precision=highest_precision)
    sine = jnp.dot(jnp.sin(angle), onehot, precision=highest_precision)
    scale = 2.0 / NT
    forward_table = jnp.stack([cosine, -sine], axis=2).reshape(NT, 2 * total_slots)
    inverse_table = jnp.stack([cosine.T * scale, -(sine.T * scale)], axis=1).reshape(
        2 * total_slots, NT
    )
    return (forward_table, inverse_table)


def convolve_pairs(spectrum, kernel_view):

    def product(left, right):
        return jnp.einsum("edcvr,cfsdr->efcvs", left, right, precision=highest_precision)

    real_out = product(spectrum[:, :, :, 0], kernel_view[:, 0]) - product(
        spectrum[:, :, :, 1], kernel_view[:, 1]
    )
    imag_out = product(spectrum[:, :, :, 1], kernel_view[:, 0]) + product(
        spectrum[:, :, :, 0], kernel_view[:, 1]
    )
    return jnp.stack([real_out, imag_out], axis=3)


def correlate_pairs(spectrum, kernel_view):

    def product(left, right):
        return jnp.einsum("efcvr,cfrdq->edcvq", left, right, precision=highest_precision)

    real_out = product(spectrum[:, :, :, 0], kernel_view[:, 0]) + product(
        spectrum[:, :, :, 1], kernel_view[:, 1]
    )
    imag_out = product(spectrum[:, :, :, 1], kernel_view[:, 0]) - product(
        spectrum[:, :, :, 0], kernel_view[:, 1]
    )
    return jnp.stack([real_out, imag_out], axis=3)


def local_general(first_field, onset, kernel, bin_owner):
    slots_here = kernel.shape[0]
    freq_count = lax.axis_size("freq")
    src_count = lax.axis_size("src")
    sub_blocks = freq_count // src_count
    total_slots = slots_here * freq_count
    forward_table, inverse_table = slot_tables(bin_owner, slots_here, total_slots)
    points = first_field.shape[0]
    traces = first_field.shape[1]
    kernel_view = kernel.reshape(slots_here, 2, sub_blocks, traces, freq_count, traces)
    sample = jnp.arange(NT, dtype=jnp.int32)
    keep = (sample[None, None, :] < onset[:, :, None]).astype(jnp.float32)

    def to_bins(field):
        spectrum = jnp.einsum("vrt,tc->cvr", field, forward_table, precision=highest_precision)
        spectrum = spectrum.reshape(freq_count, slots_here, 2, points, traces)
        return lax.all_to_all(spectrum, "freq", split_axis=0, concat_axis=0, tiled=True)

    def to_time(spectrum):
        regrouped = lax.all_to_all(spectrum, "freq", split_axis=0, concat_axis=0, tiled=True)
        flat = regrouped.reshape(2 * total_slots, points, traces)
        return jnp.einsum("cvr,ct->vrt", flat, inverse_table, precision=highest_precision)

    def widen(spectrum):
        return lax.all_gather(spectrum[None], "src", axis=0, tiled=True)

    focusing = first_field
    for sweep in range(ITERS):
        widened = widen(to_bins(focusing))
        direct = convolve_pairs(widened, kernel_view)
        direct = lax.all_to_all(direct, "src", split_axis=0, concat_axis=0, tiled=True)
        direct = direct.reshape(freq_count, slots_here, 2, points, traces)
        down = keep * to_time(direct)
        spectrum = to_bins(down)
        local_part = lax.dynamic_slice_in_dim(
            widen(spectrum), lax.axis_index("src") * sub_blocks, sub_blocks, 1
        )
        partial_terms = correlate_pairs(local_part, kernel_view)
        summed = lax.psum_scatter(partial_terms, "src", scatter_dimension=0, tiled=True)
        summed = summed.reshape(freq_count, slots_here, 2, points, traces)
        focusing = first_field + keep * to_time(summed)
    return focusing


def split(x):
    high = x.astype(BF16)
    return high, (x - high.astype(F32)).astype(BF16)


def stacked_split(x):
    high, low = split(x)
    return jnp.concatenate([high.astype(F32), low.astype(F32)], axis=0).astype(BF16)


def dot_nt(a, b):
    return lax.dot_general(a, b, (((1,), (1,)), ((), ())), preferred_element_type=F32)


def dot_nn(a, b):
    return lax.dot_general(a, b, (((1,), (0,)), ((), ())), preferred_element_type=F32)


def dot_tn(a, b):
    return lax.dot_general(a, b, (((0,), (0,)), ((), ())), preferred_element_type=F32)


def three_products(dot, both, high, low):
    rows = both.shape[0] // 2
    p = dot(both, high)
    return p[:rows] + p[rows:] + dot(both[:rows], low)


def tables(bin_owner, me, slots, freqs):
    owner = jnp.bitwise_xor(me, jnp.arange(freqs, dtype=jnp.int32))
    start = jnp.sum((bin_owner[None, :] < owner[:, None]).astype(jnp.int32), axis=1)
    count = jnp.sum((bin_owner[None, :] == owner[:, None]).astype(jnp.int32), axis=1)
    slot = jnp.arange(slots, dtype=jnp.int32)
    index = start[:, None] + slot[None, :] + FIRST_BIN
    valid = slot[None, :] < count[:, None]
    sample = jnp.arange(NT, dtype=jnp.int32)
    phase = index[:, :, None] * sample % NT
    angle = phase.astype(F32) * (2.0 * math.pi / NT)
    pair = jnp.stack([jnp.cos(angle), -jnp.sin(angle)], axis=2)
    return jnp.where(valid[:, :, None, None], pair, 0.0).reshape(freqs * slots * 2, NT)


def OUT(shape):
    return pltpu.VMEM(shape.shape, shape.dtype)


ON_CHIP = pl.BlockSpec(memory_space=pltpu.VMEM)


def on_chip(values):
    return [pltpu.with_memory_space_constraint(value, pltpu.VMEM) for value in values]


def load(kernel, place):
    slots, pair, sources, line = kernel.shape
    quarter = sources // 2
    shape = (pair, quarter, line)

    def body(place_ref, k, *refs):
        highs, lows, (done_ref, buffer, sems) = refs[:slots], refs[slots:-3], refs[-3:]
        done_ref[...] = jnp.zeros_like(done_ref)

        def copy(n):
            rows = pl.ds(pl.multiple_of(place_ref[1] * quarter, 8), quarter)
            source = k.at[n // pair, n % pair, rows, :]
            return pltpu.make_async_copy(source, buffer.at[n % 3], sems.at[n % 3])

        copy(0).start()
        copy(1).start()
        for n in range(slots * pair):
            if n + 2 < slots * pair:
                copy(n + 2).start()
            copy(n).wait()
            high, low = split(buffer[n % 3])
            highs[n // pair][n % pair] = high
            lows[n // pair][n % pair] = low

    *halves, loaded = pl.pallas_call(
        body,
        in_specs=[pl.BlockSpec(memory_space=pltpu.SMEM), pl.BlockSpec(memory_space=pl.ANY)],
        out_specs=[ON_CHIP] * (2 * slots + 1),
        out_shape=[pltpu.VMEM(shape, BF16)] * (2 * slots) + [pltpu.VMEM((8, 128), F32)],
        scratch_shapes=[pltpu.VMEM((3, quarter, line), F32), pltpu.SemaphoreType.DMA((3,))],
        compiler_params=pltpu.CompilerParams(vmem_limit_bytes=LIMIT),
    )(place, kernel)
    return halves[:slots], halves[slots:], loaded


def whole(shape):
    zeros = (0,) * len(shape)
    return pl.BlockSpec(shape, lambda *_: zeros)


def field_copy(source, field, sems, v):
    return pltpu.make_async_copy(source.at[v], field.at[v], sems.at[v])


def spectrum_kernel(points, parts, source, table, *rest):
    outs, (scratch, both, field, sems) = rest[:-4], rest[-4:]
    v = pl.program_id(0)

    @pl.when(v == 0)
    def _():
        for p in range(points):
            field_copy(source, field, sems, p).start()
        both[...] = stacked_split(table[...])

    rows = table.shape[0]
    field_copy(source, field, sems, v).wait()
    high, low = split(field[v])
    p = dot_nt(both[...], high)
    s = p[:rows] + p[rows:] + dot_nt(table[...].astype(BF16), low)
    set_point(scratch, v, points, s)

    @pl.when(v == points - 1)
    def _():
        put_pieces(scratch, outs, points, parts)


def set_point(scratch, v, points, value):
    for i in range(scratch.shape[0]):
        scratch[i, pl.ds(v, value.shape[0], stride=points), :] = value[:, 128 * i : 128 * i + 128]


def get_point(scratch, v, points):
    tiles = range(scratch.shape[0])
    rows = scratch.shape[1] // points
    return jnp.concatenate([scratch[i, pl.ds(v, rows, stride=points), :] for i in tiles], axis=1)


def rows_scratch(rows, traces):
    return pltpu.VMEM((traces // 128, rows, 128), F32)


def put_pieces(scratch, outs, points, parts, extra=None):
    height = 2 * points
    row = 0
    slots = sum(parts)
    for k in range(4):
        done = 0
        for n, size in enumerate(parts):
            for j in range(size):
                row = (k * slots + done + j) * height
                for i in range(scratch.shape[0]):
                    lanes = slice(128 * i, 128 * i + 128)
                    value = scratch[i, row : row + height, :]
                    if extra is not None:
                        value = value + extra[k][done + j, :, lanes]
                    outs[4 * n + k][j, :, lanes] = value
            done += size


def take_pieces(scratch, ins, points, parts):
    height = 2 * points
    slots = sum(parts)
    for k in range(4):
        done = 0
        for n, size in enumerate(parts):
            for j in range(size):
                row = (k * slots + done + j) * height
                for i in range(scratch.shape[0]):
                    lanes = slice(128 * i, 128 * i + 128)
                    scratch[i, row : row + height, :] = ins[4 * n + k][j, :, lanes]
            done += size


def piece_shapes(parts, height, traces):
    return [jax.ShapeDtypeStruct((size, height, traces), F32) for size in parts for _ in range(4)]


def field_scratch(field):
    return [pltpu.VMEM(field.shape, F32), pltpu.SemaphoreType.DMA((field.shape[0],))]


def spectrum(field, table, parts):
    points, traces, _ = field.shape
    rows = table.shape[0]
    shapes = piece_shapes(parts, 2 * points, traces)

    def kernel(*refs):
        spectrum_kernel(points, parts, *refs)

    return pl.pallas_call(
        kernel,
        grid=(points,),
        in_specs=[pl.BlockSpec(memory_space=pl.ANY), whole(table.shape)],
        out_specs=[whole(s.shape) for s in shapes],
        out_shape=shapes,
        scratch_shapes=[rows_scratch(rows * points, traces), pltpu.VMEM((2 * rows, NT), BF16)]
        + field_scratch(field),
        compiler_params=pltpu.CompilerParams(vmem_limit_bytes=LIMIT),
    )(pltpu.with_memory_space_constraint(field, pltpu.HBM), table)


def inverse_factor(table):
    high, low = split(table * (2.0 / NT))
    high, low = high.astype(F32), low.astype(F32)
    return jnp.concatenate([high, low, high], axis=0)


def field_factor(x):
    high, low = split(x)
    high, low = high.astype(F32), low.astype(F32)
    return jnp.concatenate([high, high, low], axis=0).astype(BF16)


def window(pieces, table, onset, parts, parts_out, extra=None):
    points, traces = onset.shape
    rows = table.shape[0]
    shapes = piece_shapes(parts_out, 2 * points, traces)
    count = len(pieces)
    extra = list(extra) if extra is not None else []

    def kernel(*refs):
        ins, refs = refs[:count], refs[count:]
        more, refs = refs[: len(extra)], refs[len(extra) :]
        table_ref, onset_ref = refs[:2]
        outs, (x_scratch, y_scratch) = refs[2:-2], refs[-2:]
        take_pieces(x_scratch, ins, points, parts)
        forward = stacked_split(table_ref[...])
        back = inverse_factor(table_ref[...]).T.astype(BF16)
        sample = lax.broadcasted_iota(jnp.int32, (NT, traces), 0)
        for v in range(points):
            x = field_factor(get_point(x_scratch, v, points))
            down = jnp.where(sample < onset_ref[v : v + 1, :], dot_nn(back, x), 0.0)
            set_point(y_scratch, v, points, transform(forward, table_ref, down))
        put_pieces(y_scratch, outs, points, parts_out, more if extra else None)

    def transform(forward, table_ref, down):
        high, low = split(down)
        p = dot_nn(forward, high)
        return p[:rows] + p[rows:] + dot_nn(table_ref[...].astype(BF16), low)

    return pl.pallas_call(
        kernel,
        in_specs=[ON_CHIP] * (count + len(extra) + 2),
        out_specs=[ON_CHIP] * len(shapes),
        out_shape=[OUT(s) for s in shapes],
        scratch_shapes=[rows_scratch(rows * points, traces)] * 2,
        compiler_params=pltpu.CompilerParams(vmem_limit_bytes=LIMIT),
    )(*on_chip([*pieces, *extra, table, onset]))


def finish(pieces, table, onset, field, parts):
    points, traces = onset.shape
    rows = table.shape[0]
    count = len(pieces)

    def kernel(*refs):
        ins = refs[:count]
        table_ref, onset_ref, source, out_ref, scratch, factor, held, sems = refs[count:]
        v = pl.program_id(0)

        @pl.when(v == 0)
        def _():
            for p in range(points):
                field_copy(source, held, sems, p).start()
            take_pieces(scratch, ins, points, parts)
            factor[...] = inverse_factor(table_ref[...]).astype(BF16)

        x = field_factor(get_point(scratch, v, points))
        g = dot_tn(x, factor[...])
        sample = lax.broadcasted_iota(jnp.int32, (traces, NT), 1)
        field_copy(source, held, sems, v).wait()
        out_ref[0] = held[v] + jnp.where(sample < onset_ref[0], g, 0.0)

    block = pl.BlockSpec((1, traces, NT), lambda v: (v, 0, 0))
    return pl.pallas_call(
        kernel,
        grid=(points,),
        in_specs=[whole(p.shape) for p in pieces]
        + [whole(table.shape), pl.BlockSpec((1, traces, 1), lambda v: (v, 0, 0)), pl.BlockSpec(memory_space=pl.ANY)],
        out_specs=block,
        out_shape=jax.ShapeDtypeStruct(field.shape, F32),
        scratch_shapes=[rows_scratch(rows * points, traces), pltpu.VMEM((3 * rows, NT), BF16)]
        + field_scratch(field),
        compiler_params=pltpu.CompilerParams(vmem_limit_bytes=LIMIT),
    )(*pieces, table, onset[:, :, None], pltpu.with_memory_space_constraint(field, pltpu.HBM))


def put_rows(both, both_turned, at, lanes, piece, sign):
    half = piece.shape[0] // 2
    rows = both.shape[0] // 2
    re, im = piece[:half], piece[half:]
    turned = jnp.concatenate([-im, re] if sign > 0 else [im, -re], axis=0)
    for target, value in ((both, piece), (both_turned, turned)):
        high, low = split(value)
        target[pl.ds(at, 2 * half), lanes] = high
        target[pl.ds(pl.multiple_of(rows + at, 16), 2 * half), lanes] = low


def convolve(partners, high, low, place):
    _, slots, height, traces = partners[0].shape
    quarter, line = high[0].shape[1:]

    def body(place_ref, a, b, c, d, *rest):
        highs, lows, rest = rest[:slots], rest[slots : 2 * slots], rest[2 * slots :]
        outs, (both, turned, g) = rest[:4], rest[4:]
        me = place_ref[0]
        for j in range(slots):
            for i in range(4):
                lanes = pl.ds(pl.multiple_of((me ^ i) * traces, 128), traces)
                for p, ref in enumerate((a, b, c, d)):
                    put_rows(both.at[j % 2], turned.at[j % 2], p * height, lanes, ref[i, j], 1)
            g[j % 2] = three_products(dot_nt, both[j % 2], highs[j][0], lows[j][0]) + three_products(
                dot_nt, turned[j % 2], highs[j][1], lows[j][1]
            )
            for i in range(4):
                outs[i][j] = g[j % 2, pl.ds(pl.multiple_of((me ^ i) * height, 16), height), :]

    shape = jax.ShapeDtypeStruct((slots, height, quarter), F32)
    return pl.pallas_call(
        body,
        in_specs=[pl.BlockSpec(memory_space=pltpu.SMEM)] + [ON_CHIP] * (4 + 2 * slots),
        out_specs=[ON_CHIP] * 4,
        out_shape=[OUT(shape)] * 4,
        scratch_shapes=[
            pltpu.VMEM((2, 8 * height, line), BF16),
            pltpu.VMEM((2, 8 * height, line), BF16),
            pltpu.VMEM((2, 4 * height, quarter), F32),
        ],
        compiler_params=pltpu.CompilerParams(vmem_limit_bytes=LIMIT),
    )(place, *on_chip([*partners, *high, *low]))


def correlate(pieces, high, low, place, offset, traces):
    slots = len(high)
    _, height, quarter = pieces[0].shape
    line = high[0].shape[2]

    def body(place_ref, a, b, c, d, *rest):
        highs, lows, rest = rest[:slots], rest[slots : 2 * slots], rest[2 * slots :]
        own, other, sibling, both, turned, h = rest
        me = place_ref[0]
        for j in range(slots):
            for i, ref in enumerate((a, b, c, d)):
                at = pl.multiple_of((me ^ i) * height, 16)
                put_rows(both.at[j % 2], turned.at[j % 2], at, slice(None), ref[j + offset], -1)
            h[j % 2] = three_products(dot_nn, both[j % 2], highs[j][0], lows[j][0]) + three_products(
                dot_nn, turned[j % 2], highs[j][1], lows[j][1]
            )
            for i in range(4):
                lanes = pl.ds(pl.multiple_of((me ^ i) * traces, 128), traces)
                own[i, j] = h[j % 2, :height, lanes]
                other[i, j] = h[j % 2, height : 2 * height, lanes]
                sibling[0, i, j] = h[j % 2, 2 * height : 3 * height, lanes]
                sibling[1, i, j] = h[j % 2, 3 * height :, lanes]

    one = jax.ShapeDtypeStruct((4, slots, height, traces), F32)
    two = jax.ShapeDtypeStruct((2, 4, slots, height, traces), F32)
    return pl.pallas_call(
        body,
        in_specs=[pl.BlockSpec(memory_space=pltpu.SMEM)] + [ON_CHIP] * (4 + 2 * slots),
        out_specs=[ON_CHIP] * 3,
        out_shape=[OUT(one), OUT(one), OUT(two)],
        scratch_shapes=[
            pltpu.VMEM((2, 8 * height, quarter), BF16),
            pltpu.VMEM((2, 8 * height, quarter), BF16),
            pltpu.VMEM((2, 4 * height, line), F32),
        ],
        compiler_params=pltpu.CompilerParams(vmem_limit_bytes=LIMIT),
    )(place, *on_chip([*pieces, *high, *low]))


def exchange(pieces):
    out = list(pieces)
    for k in (3, 2, 1):
        out[k] = lax.ppermute(pieces[k], "freq", [(f, f ^ k) for f in range(4)])
    return out


def swap(x, axis):
    return lax.ppermute(x, axis, [(0, 1), (1, 0)])


def after(value, earlier):
    value, *earlier = lax.optimization_barrier((value, *earlier))
    return value, earlier


def local_kernels(first_field, onset, kernel, bin_owner):
    slots = kernel.shape[0]
    traces = first_field.shape[1]
    parts = [slots // PARTS + (n < slots % PARTS) for n in range(PARTS)]
    offsets = [sum(parts[:n]) for n in range(PARTS)]
    me = lax.axis_index("freq").astype(jnp.int32)
    core = lax.axis_index("vp").astype(jnp.int32)
    place = jnp.stack([me, core])
    table = tables(bin_owner, me, slots, 4)
    moves = []
    for f in range(4):
        for x in range(2):
            for c in range(2):
                source = ((2 * x + c) * 2 + (x ^ (f & 1))) * 2 + (c ^ (f >> 1))
                moves.append((source, (f * 2 + x) * 2 + c))
    onset_inner = lax.ppermute(onset, ("freq", "src", "vp"), moves)

    def part_of(pieces, n):
        return pieces[4 * n : 4 * n + 4]

    def kernel_part(n):
        part = slice(offsets[n], offsets[n] + parts[n])
        return high[part], low[part]

    def conv_all(pieces, loaded):
        owns = []
        if loaded is not None:
            ready = exchange(pieces)
            for start, size in zip(offsets, parts):
                part = [piece[start : start + size] for piece in ready]
                part[1], _ = after(part[1], [loaded])
                owns.append(jnp.stack(part))
        else:
            for n in range(PARTS):
                owns.append(jnp.stack(exchange(part_of(pieces, n))))
        out, last = [], None
        for n, own in enumerate(owns):
            other = swap(own, "src")
            sibling = swap(own, "vp")
            if last is not None:
                other, last = after(other, last)
                out[-4:] = last
            across = swap(other, "vp")
            last = convolve((own, other, sibling, across), *kernel_part(n), place)
            out += last
        done = []
        for n in range(PARTS):
            done += exchange(out[4 * n : 4 * n + 4])
        return done

    def corr_all(pieces):
        ready = exchange(pieces)
        sums, turn = [], place
        for n in range(PARTS):
            own, other, sibling = correlate(ready, *kernel_part(n), turn, offsets[n], traces)
            from_sibling = swap(sibling, "vp")
            other = other + from_sibling[1]
            turn, (other,) = after(turn, [other])
            sums.append((own, from_sibling[0], swap(other, "src")))
        done = []
        for own, mine, other in sums:
            total = own + mine + other
            done += exchange([total[k] for k in range(4)])
        return done

    first = spectrum(first_field, table, [slots])
    high, low, loaded = load(kernel, place)
    pieces = first
    for sweep in range(ITERS):
        out = conv_all(pieces, loaded if sweep == 0 else None)
        out = corr_all(window(out, table, onset_inner, parts, [slots]))
        if sweep < ITERS - 1:
            pieces = window(out, table, onset, parts, parts, first)
    return finish(out, table, onset, first_field, parts)


def local(first_field, onset, kernel, bin_owner):
    points, traces, samples = first_field.shape
    quarter = kernel.shape[2] // lax.axis_size("vp")
    sizes = tuple(lax.axis_size(name) for name in ("freq", "src", "vp"))
    fits = sizes == (4, 2, 2) and points == 8 and samples == NT
    if fits and traces % 128 == 0 and quarter == traces and kernel.shape[3] == 4 * traces:
        return local_kernels(first_field, onset, kernel, bin_owner)
    return local_general(first_field, onset, kernel, bin_owner)


def solution(mesh):
    in_specs = (
        P(("groups", "src", "vp"), "freq", None),
        P(("groups", "src", "vp"), "freq"),
        P(("groups", "freq"), None, "src", None),
        P(),
    )
    out_specs = P(("groups", "src", "vp"), "freq", None)
    return jax.shard_map(local, mesh=mesh, in_specs=in_specs, out_specs=out_specs, check_vma=False)
```
